32 devices in a mesh: segment: 8 (over y, x, core), band: 4 (over z).
Axes of the slice: x: 2, y: 2, z: 4, core: 2. Of those that a mesh axis runs over, the one named last changes fastest.
Arguments:
- pixels: bfloat16 [2, 16, 16, 256], P(None, 'band'), may hold values from -6 to 6
- conv_weight: bfloat16 [8, 4, 3, 3, 256, 256], P('segment'), may hold values from -0.1875 to 0.1875
- join_weight: bfloat16 [8, 256, 256], P('segment'), may hold values from -0.25 to 0.25
Outputs:
- decoded: bfloat16 [2, 16, 16, 256], P(None, 'band', 'segment')
The draws below stay inside these ranges and needn't reach their ends.
All inputs are finite; a program needn't handle non-finite values.
Results may differ from the reference program's by a relative error of at most 0.024.
Values may be sent and summed in bfloat16 or wider, within the bound.
A program may use at most 64 MiB of HBM per device.

```python
import jax
import jax.numpy as jnp
from jax import lax

C = 256
CONVS = 4
MICRO = 2
COLS = 16
SECTIONS = 8
H = 16
N_SEGMENT = 8


def level_of(key, dims, pieces, low, top_value):
    def one(dim, parts):
        steps = jax.random.uniform(jax.random.fold_in(jax.random.fold_in(key, 6), dim), (parts,), jnp.float32, low / len(pieces), top_value / len(pieces))
        return jnp.repeat(jnp.exp(steps), dims[dim] // parts).reshape((-1,) + (1,) * (len(dims) - dim - 1))

    loudness = one(*pieces[0])
    for cut in pieces[1:]:
        loudness = loudness * one(*cut)
    return loudness


def scatter_about(own_key, shape, width, most, shards=(), kind=jnp.bfloat16):
    drawn = jax.random.normal(own_key, shape, jnp.float32) * width
    if len(shards) > 0:
        drawn = level_of(own_key, shape, shards, -0.22, 0.18) * drawn
    return jnp.clip(drawn, min=-most, max=most).astype(kind)


def setup_inputs(seed: int = 0) -> dict:
    keys = jax.random.split(jax.random.key(seed), 4)
    return {
        "pixels": scatter_about(keys[0], (MICRO, H, COLS, C), 1.0, 6.0, ((1, 4),)),
        "conv_weight": scatter_about(keys[1], (SECTIONS, CONVS, 3, 3, C, C), (9 * C // 2) ** -0.5, 0.1875, ((0, 8),)),
        "join_weight": scatter_about(keys[2], (SECTIONS, C, C), (2 * C) ** -0.5, 0.25, ((0, 8),)),
    }


def normed(hidden):
    values = hidden.astype(jnp.float32)
    scale = lax.rsqrt(lax.optimization_barrier(jnp.mean(values * values, axis=-1, keepdims=True)) + 1e-05)
    return (values * scale).astype(jnp.bfloat16)

def convolve(hidden, kernel):
    result = lax.conv_general_dilated(normed(hidden).astype(jnp.float32), kernel.astype(jnp.float32), (1, 1), ((1, 1), (1, 1)), dimension_numbers=('NHWC', 'HWIO', 'NHWC'), precision=lax.Precision.HIGHEST)
    return (hidden.astype(jnp.float32) + jnp.maximum(result, 0.0)).astype(jnp.bfloat16)

def project(hidden, weight):
    return jnp.einsum('mhwc,cd->mhwd', hidden.astype(jnp.float32), weight.astype(jnp.float32), precision=lax.Precision.HIGHEST)

def reference(pixels, conv_weight, join_weight):
    halfway = N_SEGMENT // 2
    hidden = pixels
    mirrors = []
    for section in range(N_SEGMENT):
        if section >= halfway:
            partner = N_SEGMENT - 1 - section
            hidden = (project(mirrors[partner], join_weight[partner]) + project(hidden, join_weight[section])).astype(jnp.bfloat16)
        for layer in range(CONVS):
            hidden = convolve(hidden, conv_weight[section, layer])
        if section < halfway:
            mirrors.append(hidden)
    return normed(hidden)
```

```python
import functools

import jax
import jax.numpy as jnp
from jax import lax
from jax.experimental import pallas as pl
from jax.experimental.pallas import tpu as pltpu
from jax.sharding import PartitionSpec as P

MESH = pl.DeviceIdType.MESH
HALVES = 2


def unit(values):
    return values * lax.rsqrt(jnp.mean(values * values, axis=-1, keepdims=True) + 1e-05)


def kernel(
    segments,
    bands,
    pix_ref,
    conv_ref,
    join_ref,
    out_ref,
    pix_buf,
    in_buf,
    skip_buf,
    weight_buf,
    own_join,
    mirror_join,
    skip_part,
    own_out,
    halo_out,
    place,
    fin_src,
    fin_dst,
    weight_sem,
    join_sem,
    pix_send,
    pix_recv,
    in_send,
    in_recv,
    skip_send,
    skip_recv,
    mirror_send,
    mirror_recv,
    fin_send,
    fin_recv,
):
    batches, band_rows, columns, channels = pix_ref.shape
    layers = conv_ref.shape[0]
    workers = HALVES * batches
    chunks = pix_buf.shape[0]
    own_px = own_out.shape[0]
    halo_px = halo_out.shape[0]
    half_bands = bands // HALVES
    halfway = segments // 2
    last = segments - 1
    share = columns // segments
    seg = lax.axis_index("segment")
    band = lax.axis_index("band")
    lower = lax.rem(band, HALVES)
    micro = lax.div(band, HALVES)
    other = band + 1 - 2 * lower
    works = band < workers
    own_half = lax.div(band, half_bands)

    weight_copies = []
    for layer in range(layers):
        for dy in range(3):
            to = dy + lower * (2 - 2 * dy)
            weight_copies.append(
                pltpu.make_async_copy(
                    conv_ref.at[layer, dy], weight_buf.at[layer, to], weight_sem.at[layer, dy]
                )
            )
    join_copy = pltpu.make_async_copy(join_ref, own_join, join_sem)

    @pl.when(works)
    def _():
        for copy in weight_copies:
            copy.start()
        join_copy.start()

    barrier = pltpu.get_barrier_semaphore()

    def greet(to_seg, to_band):
        pl.semaphore_signal(barrier, inc=1, device_id=(to_seg, to_band), device_id_type=MESH)

    def chunk_band(chunk):
        return chunk + lower * (bands - 1 - 2 * chunk)

    @pl.when(works & (seg == 0))
    def _():
        for chunk in range(chunks):

            @pl.when(chunk_band(chunk) != band)
            def _():
                greet(0, chunk_band(chunk))

    @pl.when(works & (seg > 0))
    def _():
        greet(seg - 1, band)
        greet(seg - 1, other)

    @pl.when(works & (seg > halfway))
    def _():
        greet(last - seg, band)
        greet(last - seg, other)

    for m in range(batches):

        @pl.when((seg != last) | (band != HALVES * m + own_half))
        def _():
            greet(last, HALVES * m + own_half)

    def one_if(condition):
        return jnp.where(condition, 1, 0).astype(jnp.int32)

    def pix_chunk(worker):
        return band if worker % HALVES == 0 else bands - 1 - band

    def pix_sends(worker):
        return (seg == 0) & (pix_chunk(worker) < chunks) & (band != worker)

    expected = one_if(works & (seg < last)) * 2 + one_if(works & (seg < halfway - 1)) * 2
    for worker in range(workers):
        expected += one_if(pix_sends(worker))
    expected += one_if(works & (seg == last)) * (
        segments * half_bands - one_if(own_half == lower)
    )

    @pl.when(expected > 0)
    def _():
        pl.semaphore_wait(barrier, expected)

    def pix_copy(worker):
        return pltpu.make_async_remote_copy(
            src_ref=pix_ref.at[worker // HALVES],
            dst_ref=pix_buf.at[pix_chunk(worker)],
            send_sem=pix_send.at[worker],
            recv_sem=pix_recv.at[pix_chunk(worker)],
            device_id=(0, worker),
            device_id_type=MESH,
        )

    own_chunk = band + lower * (bands - 1 - 2 * band)
    for worker in range(workers):

        @pl.when(pix_sends(worker))
        def _():
            pix_copy(worker).start()

    @pl.when(works & (seg == 0) & (own_chunk < chunks))
    def _():
        pltpu.make_async_copy(
            pix_ref.at[micro], pix_buf.at[own_chunk], pix_recv.at[own_chunk]
        ).start()

    mirror_copy = pltpu.make_async_remote_copy(
        src_ref=join_ref,
        dst_ref=mirror_join,
        send_sem=mirror_send,
        recv_sem=mirror_recv,
        device_id=(last - seg, band),
        device_id_type=MESH,
    )

    @pl.when(works & (seg < halfway))
    def _():
        mirror_copy.start()

    def hop_copies(buffer, to_seg, send, recv):
        return (
            pltpu.make_async_remote_copy(
                src_ref=own_out,
                dst_ref=buffer.at[pl.ds(0, own_px)],
                send_sem=send.at[0],
                recv_sem=recv.at[0],
                device_id=(to_seg, band),
                device_id_type=MESH,
            ),
            pltpu.make_async_remote_copy(
                src_ref=halo_out,
                dst_ref=buffer.at[pl.ds(own_px, halo_px)],
                send_sem=send.at[1],
                recv_sem=recv.at[1],
                device_id=(to_seg, other),
                device_id_type=MESH,
            ),
        )

    next_copies = hop_copies(in_buf, seg + 1, in_send, in_recv)
    skip_copies = hop_copies(skip_buf, last - seg, skip_send, skip_recv)

    def fin_copy(g, k):
        return pltpu.make_async_remote_copy(
            src_ref=fin_src.at[g * half_bands + k],
            dst_ref=fin_dst.at[micro],
            send_sem=fin_send.at[g * half_bands + k],
            recv_sem=fin_recv.at[micro],
            device_id=(g, chunk_band(k)),
            device_id_type=MESH,
        )

    def dot(a, b):
        return jnp.dot(a, b, preferred_element_type=jnp.float32)

    @pl.when(works)
    def _():
        @pl.when(seg == last)
        def _():
            block_rows = fin_src.shape[1]
            at = lax.broadcasted_iota(jnp.int32, (block_rows, own_px), 0)
            pixel = lax.broadcasted_iota(jnp.int32, (block_rows, own_px), 1)
            row = jnp.zeros_like(at)
            for step in range(1, band_rows):
                row += jnp.where(at >= step * share, 1, 0)
            column = at - row * share
            row = row + lower * (band_rows - 1 - 2 * row)
            inside = at < band_rows * share
            base = row * columns + column
            for g in range(segments):
                for k in range(half_bands):
                    wanted = base + (k * band_rows * columns + g * share)
                    place[g * half_bands + k] = jnp.where(
                        inside & (pixel == wanted), 1.0, 0.0
                    ).astype(jnp.bfloat16)

        join_copy.wait()

        @pl.when(seg >= halfway)
        def _():
            mirror_copy.wait_recv()

        @pl.when(seg > halfway)
        def _():
            for copy in skip_copies:
                copy.wait_recv()
            skip_part[...] = dot(skip_buf[...], mirror_join[...])

        @pl.when(seg == 0)
        def _():
            for chunk in range(chunks):
                pltpu.make_async_copy(
                    pix_ref.at[0], pix_buf.at[chunk], pix_recv.at[chunk]
                ).wait()
            for row in range((own_px + halo_px) // columns):
                within = row % band_rows
                within = within + lower * (band_rows - 1 - 2 * within)
                in_buf[pl.ds(row * columns, columns)] = pix_buf[row // band_rows, within]

        @pl.when(seg > 0)
        def _():
            for copy in next_copies:
                copy.wait_recv()

        @pl.when(seg == halfway)
        def _():
            skip_part[...] = dot(in_buf[...], mirror_join[...])

        @pl.when(seg >= halfway)
        def _():
            in_buf[...] = (skip_part[...] + dot(in_buf[...], own_join[...])).astype(jnp.bfloat16)

        hidden = in_buf[...]
        for layer in range(layers):
            values = hidden.astype(jnp.float32)
            count = values.shape[0]
            scaled = unit(values)
            at = lax.rem(lax.broadcasted_iota(jnp.int32, (count, channels), 0), columns)
            left = jnp.where(at == 0, 0.0, pltpu.roll(scaled, 1, 0))
            right = jnp.where(at == columns - 1, 0.0, pltpu.roll(scaled, count - 1, 0))
            wide = jnp.concatenate(
                [part.astype(jnp.bfloat16) for part in (left, scaled, right)], axis=1
            )
            wide = jnp.concatenate([jnp.zeros((columns, wide.shape[1]), jnp.bfloat16), wide], axis=0)
            keep = count - columns
            for dy in range(3):
                weight_copies[layer * 3 + dy].wait()
            patches = jnp.concatenate(
                [wide[dy * columns : dy * columns + keep] for dy in range(3)], axis=1
            )
            total = dot(patches, weight_buf[layer].reshape(patches.shape[1], channels))
            hidden = (values[:keep] + jnp.maximum(total, 0.0)).astype(jnp.bfloat16)

        @pl.when(seg < last)
        def _():
            own_out[...] = hidden
            for row in range(halo_px // columns):
                start = own_px - (row + 1) * columns
                halo_out[pl.ds(row * columns, columns)] = hidden[start : start + columns]
            for copy in next_copies:
                copy.start()

            @pl.when(seg < halfway - 1)
            def _():
                for copy in skip_copies:
                    copy.start()

        @pl.when(seg == last)
        def _():
            decoded = unit(hidden.astype(jnp.float32)).astype(jnp.bfloat16)
            sorting = place[...].reshape(-1, own_px)
            fin_src[...] = dot(sorting, decoded).astype(jnp.bfloat16).reshape(fin_src.shape)
            for g in range(segments):
                for k in range(half_bands):
                    if g < last:
                        fin_copy(g, k).start()
                    else:
                        here = chunk_band(k) == band

                        @pl.when(here)
                        def _():
                            pltpu.make_async_copy(
                                fin_src.at[g * half_bands + k],
                                fin_dst.at[micro],
                                fin_recv.at[micro],
                            ).start()

                        @pl.when(jnp.logical_not(here))
                        def _():
                            fin_copy(g, k).start()

    for m in range(batches):
        pltpu.make_async_copy(fin_src.at[0], fin_dst.at[m], fin_recv.at[m]).wait()
    out_ref[...] = fin_dst[...]

    for worker in range(workers):

        @pl.when(pix_sends(worker))
        def _():
            pix_copy(worker).wait_send()

    @pl.when(works & (seg < halfway))
    def _():
        mirror_copy.wait_send()

    @pl.when(works & (seg < last))
    def _():
        for copy in next_copies:
            copy.wait_send()

    @pl.when(works & (seg < halfway - 1))
    def _():
        for copy in skip_copies:
            copy.wait_send()

    @pl.when(works & (seg == last))
    def _():
        for g in range(segments):
            for k in range(half_bands):
                if g < last:
                    fin_copy(g, k).wait_send()
                else:

                    @pl.when(chunk_band(k) != band)
                    def _():
                        fin_copy(g, k).wait_send()


def shards(segments, bands, pixels, conv_weight, join_weight):
    batches, band_rows, columns, channels = pixels.shape
    layers = conv_weight.shape[1]
    own_rows = band_rows * bands // HALVES
    rows = own_rows + layers
    chunks = -(-rows // band_rows)
    own_px, halo_px, all_px = own_rows * columns, layers * columns, rows * columns
    share = columns // segments
    piece = band_rows * share
    block_rows = -(-piece // 16) * 16
    blocks = segments * (bands // HALVES)
    workers = HALVES * batches
    kept = jnp.bfloat16
    conv = conv_weight.reshape(layers, 3, 3 * channels, channels)
    join = join_weight.reshape(channels, channels)
    dma = pltpu.SemaphoreType.DMA
    result = pl.pallas_call(
        functools.partial(kernel, segments, bands),
        out_shape=jax.ShapeDtypeStruct((batches, block_rows, channels), kept),
        in_specs=[pl.BlockSpec(memory_space=pl.ANY)] * 3,
        out_specs=pl.BlockSpec(memory_space=pltpu.VMEM),
        scratch_shapes=[
            pltpu.VMEM((chunks, band_rows, columns, channels), kept),
            pltpu.VMEM((all_px, channels), kept),
            pltpu.VMEM((all_px, channels), kept),
            pltpu.VMEM((layers, 3, 3 * channels, channels), kept),
            pltpu.VMEM((channels, channels), kept),
            pltpu.VMEM((channels, channels), kept),
            pltpu.VMEM((all_px, channels), jnp.float32),
            pltpu.VMEM((own_px, channels), kept),
            pltpu.VMEM((halo_px, channels), kept),
            pltpu.VMEM((blocks, block_rows, own_px), kept),
            pltpu.VMEM((blocks, block_rows, channels), kept),
            pltpu.VMEM((batches, block_rows, channels), kept),
            dma((layers, 3)),
            dma,
            dma((workers,)),
            dma((chunks,)),
            dma((2,)),
            dma((2,)),
            dma((2,)),
            dma((2,)),
            dma,
            dma,
            dma((blocks,)),
            dma((batches,)),
        ],
        compiler_params=pltpu.CompilerParams(
            collective_id=0, has_side_effects=True, vmem_limit_bytes=40 * 1024 * 1024
        ),
    )(pixels, conv, join)
    return result[:, :piece].reshape(batches, band_rows, share, channels)


def solution(mesh):
    return jax.shard_map(
        functools.partial(shards, mesh.shape["segment"], mesh.shape["band"]),
        mesh=mesh,
        in_specs=(
            P(None, "band", None, None),
            P("segment", None, None, None, None, None),
            P("segment", None, None),
        ),
        out_specs=P(None, "band", "segment", None),
        check_vma=False,
    )
```

```python
import functools

import jax
import jax.numpy as jnp
from jax import lax
from jax.experimental import pallas as pl
from jax.experimental.pallas import tpu as pltpu
from jax.sharding import PartitionSpec as P

MESH = pl.DeviceIdType.MESH
HALVES = 2


def unit(values):
    return values * lax.rsqrt(jnp.mean(values * values, axis=-1, keepdims=True) + 1e-05)


def kernel(
    segments,
    bands,
    pix_ref,
    conv_ref,
    join_ref,
    out_ref,
    pix_buf,
    in_buf,
    skip_buf,
    weight_buf,
    own_join,
    mirror_join,
    skip_part,
    own_out,
    halo_out,
    place,
    fin_src,
    fin_dst,
    weight_sem,
    join_sem,
    pix_send,
    pix_recv,
    in_send,
    in_recv,
    skip_send,
    skip_recv,
    mirror_send,
    mirror_recv,
    fin_send,
    fin_recv,
):
    batches, band_rows, columns, channels = pix_ref.shape
    layers = conv_ref.shape[0]
    workers = HALVES * batches
    chunks = pix_buf.shape[0]
    own_px = own_out.shape[0]
    halo_px = halo_out.shape[0]
    half_bands = bands // HALVES
    halfway = segments // 2
    last = segments - 1
    share = columns // segments
    seg = lax.axis_index("segment")
    band = lax.axis_index("band")
    lower = lax.rem(band, HALVES)
    micro = lax.div(band, HALVES)
    other = band + 1 - 2 * lower
    works = band < workers
    own_half = lax.div(band, half_bands)

    weight_copies = []
    for layer in range(layers):
        for dy in range(3):
            to = dy + lower * (2 - 2 * dy)
            weight_copies.append(
                pltpu.make_async_copy(
                    conv_ref.at[layer, dy], weight_buf.at[layer, to], weight_sem.at[layer, dy]
                )
            )
    join_copy = pltpu.make_async_copy(join_ref, own_join, join_sem)

    @pl.when(works)
    def _():
        for copy in weight_copies:
            copy.start()
        join_copy.start()

    barrier = pltpu.get_barrier_semaphore()

    def greet(to_seg, to_band):
        pl.semaphore_signal(barrier, inc=1, device_id=(to_seg, to_band), device_id_type=MESH)

    def chunk_band(chunk):
        return chunk + lower * (bands - 1 - 2 * chunk)

    @pl.when(works & (seg == 0))
    def _():
        for chunk in range(chunks):

            @pl.when(chunk_band(chunk) != band)
            def _():
                greet(0, chunk_band(chunk))

    @pl.when(works & (seg > 0))
    def _():
        greet(seg - 1, band)
        greet(seg - 1, other)

    @pl.when(works & (seg > halfway))
    def _():
        greet(last - seg, band)
        greet(last - seg, other)

    for m in range(batches):

        @pl.when((seg != last) | (band != HALVES * m + own_half))
        def _():
            greet(last, HALVES * m + own_half)

    def one_if(condition):
        return jnp.where(condition, 1, 0).astype(jnp.int32)

    def pix_chunk(worker):
        return band if worker % HALVES == 0 else bands - 1 - band

    def pix_sends(worker):
        return (seg == 0) & (pix_chunk(worker) < chunks) & (band != worker)

    expected = one_if(works & (seg < last)) * 2 + one_if(works & (seg < halfway - 1)) * 2
    for worker in range(workers):
        expected += one_if(pix_sends(worker))
    expected += one_if(works & (seg == last)) * (
        segments * half_bands - one_if(own_half == lower)
    )

    @pl.when(expected > 0)
    def _():
        pl.semaphore_wait(barrier, expected)

    def pix_copy(worker):
        return pltpu.make_async_remote_copy(
            src_ref=pix_ref.at[worker // HALVES],
            dst_ref=pix_buf.at[pix_chunk(worker)],
            send_sem=pix_send.at[worker],
            recv_sem=pix_recv.at[pix_chunk(worker)],
            device_id=(0, worker),
            device_id_type=MESH,
        )

    own_chunk = band + lower * (bands - 1 - 2 * band)
    for worker in range(workers):

        @pl.when(pix_sends(worker))
        def _():
            pix_copy(worker).start()

    @pl.when(works & (seg == 0) & (own_chunk < chunks))
    def _():
        pltpu.make_async_copy(
            pix_ref.at[micro], pix_buf.at[own_chunk], pix_recv.at[own_chunk]
        ).start()

    mirror_copy = pltpu.make_async_remote_copy(
        src_ref=join_ref,
        dst_ref=mirror_join,
        send_sem=mirror_send,
        recv_sem=mirror_recv,
        device_id=(last - seg, band),
        device_id_type=MESH,
    )

    @pl.when(works & (seg < halfway))
    def _():
        mirror_copy.start()

    def hop_copies(buffer, to_seg, send, recv):
        return (
            pltpu.make_async_remote_copy(
                src_ref=own_out,
                dst_ref=buffer.at[pl.ds(0, own_px)],
                send_sem=send.at[0],
                recv_sem=recv.at[0],
                device_id=(to_seg, band),
                device_id_type=MESH,
            ),
            pltpu.make_async_remote_copy(
                src_ref=halo_out,
                dst_ref=buffer.at[pl.ds(own_px, halo_px)],
                send_sem=send.at[1],
                recv_sem=recv.at[1],
                device_id=(to_seg, other),
                device_id_type=MESH,
            ),
        )

    next_copies = hop_copies(in_buf, seg + 1, in_send, in_recv)
    skip_copies = hop_copies(skip_buf, last - seg, skip_send, skip_recv)

    def fin_copy(g, k):
        return pltpu.make_async_remote_copy(
            src_ref=fin_src.at[g * half_bands + k],
            dst_ref=fin_dst.at[micro],
            send_sem=fin_send.at[g * half_bands + k],
            recv_sem=fin_recv.at[micro],
            device_id=(g, chunk_band(k)),
            device_id_type=MESH,
        )

    def dot(a, b):
        return jnp.dot(a, b, preferred_element_type=jnp.float32)

    @pl.when(works)
    def _():
        @pl.when(seg == last)
        def _():
            block_rows = fin_src.shape[1]
            at = lax.broadcasted_iota(jnp.int32, (block_rows, own_px), 0)
            pixel = lax.broadcasted_iota(jnp.int32, (block_rows, own_px), 1)
            row = jnp.zeros_like(at)
            for step in range(1, band_rows):
                row += jnp.where(at >= step * share, 1, 0)
            column = at - row * share
            row = row + lower * (band_rows - 1 - 2 * row)
            inside = at < band_rows * share
            base = row * columns + column
            for g in range(segments):
                for k in range(half_bands):
                    wanted = base + (k * band_rows * columns + g * share)
                    place[g * half_bands + k] = jnp.where(
                        inside & (pixel == wanted), 1.0, 0.0
                    ).astype(jnp.bfloat16)

        join_copy.wait()

        @pl.when(seg >= halfway)
        def _():
            mirror_copy.wait_recv()

        @pl.when(seg > halfway)
        def _():
            for copy in skip_copies:
                copy.wait_recv()
            skip_part[...] = dot(skip_buf[...], mirror_join[...])

        @pl.when(seg == 0)
        def _():
            for chunk in range(chunks):
                pltpu.make_async_copy(
                    pix_ref.at[0], pix_buf.at[chunk], pix_recv.at[chunk]
                ).wait()
            for row in range((own_px + halo_px) // columns):
                within = row % band_rows
                within = within + lower * (band_rows - 1 - 2 * within)
                in_buf[pl.ds(row * columns, columns)] = pix_buf[row // band_rows, within]

        @pl.when(seg > 0)
        def _():
            for copy in next_copies:
                copy.wait_recv()

        @pl.when(seg == halfway)
        def _():
            skip_part[...] = dot(in_buf[...], mirror_join[...])

        @pl.when(seg >= halfway)
        def _():
            in_buf[...] = (skip_part[...] + dot(in_buf[...], own_join[...])).astype(jnp.bfloat16)

        hidden = in_buf[...]
        for layer in range(layers):
            values = hidden.astype(jnp.float32)
            count = values.shape[0]
            scaled = unit(values)
            at = lax.broadcasted_iota(
                jnp.int32, (count // columns, columns, channels), 1
            ).reshape(count, channels)
            left = jnp.where(at == 0, 0.0, pltpu.roll(scaled, 1, 0))
            right = jnp.where(at == columns - 1, 0.0, pltpu.roll(scaled, count - 1, 0))
            wide = jnp.concatenate(
                [part.astype(jnp.bfloat16) for part in (left, scaled, right)], axis=1
            )
            wide = jnp.concatenate([jnp.zeros((columns, wide.shape[1]), jnp.bfloat16), wide], axis=0)
            keep = count - columns
            for dy in range(3):
                weight_copies[layer * 3 + dy].wait()
            patches = jnp.concatenate(
                [wide[dy * columns : dy * columns + keep] for dy in range(3)], axis=1
            )
            total = dot(patches, weight_buf[layer].reshape(patches.shape[1], channels))
            hidden = (values[:keep] + jnp.maximum(total, 0.0)).astype(jnp.bfloat16)

        @pl.when(seg < last)
        def _():
            own_out[...] = hidden
            for row in range(halo_px // columns):
                start = own_px - (row + 1) * columns
                halo_out[pl.ds(row * columns, columns)] = hidden[start : start + columns]
            for copy in next_copies:
                copy.start()

            @pl.when(seg < halfway - 1)
            def _():
                for copy in skip_copies:
                    copy.start()

        @pl.when(seg == last)
        def _():
            decoded = unit(hidden.astype(jnp.float32)).astype(jnp.bfloat16)
            sorting = place[...].reshape(-1, own_px)
            fin_src[...] = dot(sorting, decoded).astype(jnp.bfloat16).reshape(fin_src.shape)
            for g in range(segments):
                for k in range(half_bands):
                    if g < last:
                        fin_copy(g, k).start()
                    else:
                        here = chunk_band(k) == band

                        @pl.when(here)
                        def _():
                            pltpu.make_async_copy(
                                fin_src.at[g * half_bands + k],
                                fin_dst.at[micro],
                                fin_recv.at[micro],
                            ).start()

                        @pl.when(jnp.logical_not(here))
                        def _():
                            fin_copy(g, k).start()

    for m in range(batches):
        pltpu.make_async_copy(fin_src.at[0], fin_dst.at[m], fin_recv.at[m]).wait()
    out_ref[...] = fin_dst[...]

    for worker in range(workers):

        @pl.when(pix_sends(worker))
        def _():
            pix_copy(worker).wait_send()

    @pl.when(works & (seg < halfway))
    def _():
        mirror_copy.wait_send()

    @pl.when(works & (seg < last))
    def _():
        for copy in next_copies:
            copy.wait_send()

    @pl.when(works & (seg < halfway - 1))
    def _():
        for copy in skip_copies:
            copy.wait_send()

    @pl.when(works & (seg == last))
    def _():
        for g in range(segments):
            for k in range(half_bands):
                if g < last:
                    fin_copy(g, k).wait_send()
                else:

                    @pl.when(chunk_band(k) != band)
                    def _():
                        fin_copy(g, k).wait_send()


def shards(segments, bands, pixels, conv_weight, join_weight):
    batches, band_rows, columns, channels = pixels.shape
    layers = conv_weight.shape[1]
    own_rows = band_rows * bands // HALVES
    rows = own_rows + layers
    chunks = -(-rows // band_rows)
    own_px, halo_px, all_px = own_rows * columns, layers * columns, rows * columns
    share = columns // segments
    piece = band_rows * share
    block_rows = -(-piece // 16) * 16
    blocks = segments * (bands // HALVES)
    workers = HALVES * batches
    kept = jnp.bfloat16
    conv = conv_weight.reshape(layers, 3, 3 * channels, channels)
    join = join_weight.reshape(channels, channels)
    dma = pltpu.SemaphoreType.DMA
    result = pl.pallas_call(
        functools.partial(kernel, segments, bands),
        out_shape=jax.ShapeDtypeStruct((batches, block_rows, channels), kept),
        in_specs=[pl.BlockSpec(memory_space=pltpu.HBM)] * 3,
        out_specs=pl.BlockSpec(memory_space=pltpu.VMEM),
        scratch_shapes=[
            pltpu.VMEM((chunks, band_rows, columns, channels), kept),
            pltpu.VMEM((all_px, channels), kept),
            pltpu.VMEM((all_px, channels), kept),
            pltpu.VMEM((layers, 3, 3 * channels, channels), kept),
            pltpu.VMEM((channels, channels), kept),
            pltpu.VMEM((channels, channels), kept),
            pltpu.VMEM((all_px, channels), jnp.float32),
            pltpu.VMEM((own_px, channels), kept),
            pltpu.VMEM((halo_px, channels), kept),
            pltpu.VMEM((blocks, block_rows, own_px), kept),
            pltpu.VMEM((blocks, block_rows, channels), kept),
            pltpu.VMEM((batches, block_rows, channels), kept),
            dma((layers, 3)),
            dma,
            dma((workers,)),
            dma((chunks,)),
            dma((2,)),
            dma((2,)),
            dma((2,)),
            dma((2,)),
            dma,
            dma,
            dma((blocks,)),
            dma((batches,)),
        ],
        compiler_params=pltpu.CompilerParams(
            collective_id=0, has_side_effects=True, vmem_limit_bytes=40 * 1024 * 1024
        ),
    )(pixels, conv, join)
    return result[:, :piece].reshape(batches, band_rows, share, channels)


def solution(mesh):
    return jax.shard_map(
        functools.partial(shards, mesh.shape["segment"], mesh.shape["band"]),
        mesh=mesh,
        in_specs=(
            P(None, "band", None, None),
            P("segment", None, None, None, None, None),
            P("segment", None, None),
        ),
        out_specs=P(None, "band", "segment", None),
        check_vma=False,
    )
```

```python
import functools

import jax
import jax.numpy as jnp
from jax import lax
from jax.experimental import pallas as pl
from jax.experimental.pallas import tpu as pltpu
from jax.sharding import PartitionSpec as P

MESH = pl.DeviceIdType.MESH
HALVES = 2


def unit(values):
    return values * lax.rsqrt(jnp.mean(values * values, axis=-1, keepdims=True) + 1e-05)


def kernel(
    segments,
    bands,
    pix_ref,
    conv_ref,
    join_ref,
    out_ref,
    pix_buf,
    in_buf,
    skip_buf,
    weight_buf,
    own_join,
    mirror_join,
    skip_part,
    hid,
    wide,
    own_out,
    halo_out,
    place,
    fin_src,
    fin_dst,
    weight_sem,
    join_sem,
    pix_send,
    pix_recv,
    in_send,
    in_recv,
    skip_send,
    skip_recv,
    mirror_send,
    mirror_recv,
    fin_send,
    fin_recv,
):
    batches, band_rows, columns, channels = pix_ref.shape
    layers = conv_ref.shape[0]
    workers = HALVES * batches
    chunks = pix_buf.shape[0]
    own_px = own_out.shape[0]
    halo_px = halo_out.shape[0]
    all_px = own_px + halo_px
    half_bands = bands // HALVES
    halfway = segments // 2
    last = segments - 1
    share = columns // segments
    seg = lax.axis_index("segment")
    band = lax.axis_index("band")
    lower = lax.rem(band, HALVES)
    micro = lax.div(band, HALVES)
    other = band + 1 - 2 * lower
    works = band < workers
    own_half = lax.div(band, half_bands)

    weight_copies = []
    for layer in range(layers):
        for dy in range(3):
            to = dy + lower * (2 - 2 * dy)
            weight_copies.append(
                pltpu.make_async_copy(
                    conv_ref.at[layer, dy], weight_buf.at[layer, to], weight_sem.at[layer, dy]
                )
            )
    join_copy = pltpu.make_async_copy(join_ref, own_join, join_sem)

    @pl.when(works)
    def _():
        for copy in weight_copies:
            copy.start()
        join_copy.start()

    barrier = pltpu.get_barrier_semaphore()

    def greet(to_seg, to_band):
        pl.semaphore_signal(barrier, inc=1, device_id=(to_seg, to_band), device_id_type=MESH)

    def chunk_band(chunk):
        return chunk + lower * (bands - 1 - 2 * chunk)

    @pl.when(works & (seg == 0))
    def _():
        for chunk in range(chunks):

            @pl.when(chunk_band(chunk) != band)
            def _():
                greet(0, chunk_band(chunk))

    @pl.when(works & (seg > 0))
    def _():
        greet(seg - 1, band)
        greet(seg - 1, other)

    @pl.when(works & (seg > halfway))
    def _():
        greet(last - seg, band)
        greet(last - seg, other)

    for m in range(batches):

        @pl.when((seg != last) | (band != HALVES * m + own_half))
        def _():
            greet(last, HALVES * m + own_half)

    def one_if(condition):
        return jnp.where(condition, 1, 0).astype(jnp.int32)

    def pix_chunk(worker):
        return band if worker % HALVES == 0 else bands - 1 - band

    def pix_sends(worker):
        return (seg == 0) & (pix_chunk(worker) < chunks) & (band != worker)

    expected = one_if(works & (seg < last)) * 2 + one_if(works & (seg < halfway - 1)) * 2
    for worker in range(workers):
        expected += one_if(pix_sends(worker))
    expected += one_if(works & (seg == last)) * (
        segments * half_bands - one_if(own_half == lower)
    )

    @pl.when(expected > 0)
    def _():
        pl.semaphore_wait(barrier, expected)

    def pix_copy(worker):
        return pltpu.make_async_remote_copy(
            src_ref=pix_ref.at[worker // HALVES],
            dst_ref=pix_buf.at[pix_chunk(worker)],
            send_sem=pix_send.at[worker],
            recv_sem=pix_recv.at[pix_chunk(worker)],
            device_id=(0, worker),
            device_id_type=MESH,
        )

    own_chunk = band + lower * (bands - 1 - 2 * band)
    for worker in range(workers):

        @pl.when(pix_sends(worker))
        def _():
            pix_copy(worker).start()

    @pl.when(works & (seg == 0) & (own_chunk < chunks))
    def _():
        pltpu.make_async_copy(
            pix_ref.at[micro], pix_buf.at[own_chunk], pix_recv.at[own_chunk]
        ).start()

    mirror_copy = pltpu.make_async_remote_copy(
        src_ref=join_ref,
        dst_ref=mirror_join,
        send_sem=mirror_send,
        recv_sem=mirror_recv,
        device_id=(last - seg, band),
        device_id_type=MESH,
    )

    @pl.when(works & (seg < halfway))
    def _():
        mirror_copy.start()

    def hop_copies(buffer, to_seg, send, recv):
        return (
            pltpu.make_async_remote_copy(
                src_ref=own_out,
                dst_ref=buffer.at[pl.ds(0, own_px)],
                send_sem=send.at[0],
                recv_sem=recv.at[0],
                device_id=(to_seg, band),
                device_id_type=MESH,
            ),
            pltpu.make_async_remote_copy(
                src_ref=halo_out,
                dst_ref=buffer.at[pl.ds(own_px, halo_px)],
                send_sem=send.at[1],
                recv_sem=recv.at[1],
                device_id=(to_seg, other),
                device_id_type=MESH,
            ),
        )

    next_copies = hop_copies(in_buf, seg + 1, in_send, in_recv)
    skip_copies = hop_copies(skip_buf, last - seg, skip_send, skip_recv)

    def fin_copy(g, k):
        return pltpu.make_async_remote_copy(
            src_ref=fin_src.at[g * half_bands + k],
            dst_ref=fin_dst.at[micro],
            send_sem=fin_send.at[g * half_bands + k],
            recv_sem=fin_recv.at[micro],
            device_id=(g, chunk_band(k)),
            device_id_type=MESH,
        )

    def dot(a, b):
        return jnp.dot(a, b, preferred_element_type=jnp.float32)

    @pl.when(works)
    def _():
        @pl.when(seg == last)
        def _():
            block_rows = fin_src.shape[1]
            at = lax.broadcasted_iota(jnp.int32, (block_rows, own_px), 0)
            pixel = lax.broadcasted_iota(jnp.int32, (block_rows, own_px), 1)
            row = jnp.zeros_like(at)
            for step in range(1, band_rows):
                row += jnp.where(at >= step * share, 1, 0)
            column = at - row * share
            row = row + lower * (band_rows - 1 - 2 * row)
            inside = at < band_rows * share
            base = row * columns + column
            for g in range(segments):
                for k in range(half_bands):
                    wanted = base + (k * band_rows * columns + g * share)
                    place[g * half_bands + k] = jnp.where(
                        inside & (pixel == wanted), 1.0, 0.0
                    ).astype(jnp.bfloat16)

        hid[...] = jnp.zeros_like(hid)
        wide[pl.ds(0, columns)] = jnp.zeros((columns, wide.shape[1]), jnp.bfloat16)
        join_copy.wait()
        for copy in weight_copies:
            copy.wait()

        @pl.when(seg >= halfway)
        def _():
            mirror_copy.wait_recv()

        @pl.when(seg > halfway)
        def _():
            for copy in skip_copies:
                copy.wait_recv()
            skip_part[...] = dot(skip_buf[...], mirror_join[...])

        def take_input():
            @pl.when(seg == 0)
            def _():
                for chunk in range(chunks):
                    pltpu.make_async_copy(
                        pix_ref.at[0], pix_buf.at[chunk], pix_recv.at[chunk]
                    ).wait()
                for row in range(all_px // columns):
                    within = row % band_rows
                    within = within + lower * (band_rows - 1 - 2 * within)
                    hid[pl.ds(row * columns, columns)] = pix_buf[row // band_rows, within]

            @pl.when(seg > 0)
            def _():
                for copy in next_copies:
                    copy.wait_recv()

            @pl.when((seg > 0) & (seg < halfway))
            def _():
                hid[...] = in_buf[...]

            @pl.when(seg == halfway)
            def _():
                skip_part[...] = dot(in_buf[...], mirror_join[...])

            @pl.when(seg >= halfway)
            def _():
                hid[...] = (skip_part[...] + dot(in_buf[...], own_join[...])).astype(jnp.bfloat16)

        keep = all_px - columns
        at = lax.broadcasted_iota(jnp.int32, (all_px // columns, columns, channels), 1).reshape(
            all_px, channels
        )

        def step(index, carry):
            @pl.when(index == 1)
            def _():
                take_input()

            layer = jnp.maximum(index - 1, 0)
            scaled = unit(hid[...].astype(jnp.float32))
            left = jnp.where(at == 0, 0.0, pltpu.roll(scaled, 1, 0))
            right = jnp.where(at == columns - 1, 0.0, pltpu.roll(scaled, all_px - 1, 0))
            for place_at, part in enumerate((left, scaled, right)):
                wide[pl.ds(columns, all_px), pl.ds(place_at * channels, channels)] = part.astype(
                    jnp.bfloat16
                )
            total = dot(wide[pl.ds(0, keep)], weight_buf[layer, 0])
            for dy in range(1, 3):
                total += dot(wide[pl.ds(dy * columns, keep)], weight_buf[layer, dy])
            hid[pl.ds(0, keep)] = (
                hid[pl.ds(0, keep)].astype(jnp.float32) + jnp.maximum(total, 0.0)
            ).astype(jnp.bfloat16)
            return carry

        lax.fori_loop(0, layers + 1, step, 0)
        hidden = hid[pl.ds(0, own_px)]

        @pl.when(seg < last)
        def _():
            own_out[...] = hidden
            for row in range(halo_px // columns):
                start = own_px - (row + 1) * columns
                halo_out[pl.ds(row * columns, columns)] = hidden[start : start + columns]
            for copy in next_copies:
                copy.start()

            @pl.when(seg < halfway - 1)
            def _():
                for copy in skip_copies:
                    copy.start()

        @pl.when(seg == last)
        def _():
            decoded = unit(hidden.astype(jnp.float32)).astype(jnp.bfloat16)
            sorting = place[...].reshape(-1, own_px)
            fin_src[...] = dot(sorting, decoded).astype(jnp.bfloat16).reshape(fin_src.shape)
            for g in range(segments):
                for k in range(half_bands):
                    if g < last:
                        fin_copy(g, k).start()
                    else:
                        here = chunk_band(k) == band

                        @pl.when(here)
                        def _():
                            pltpu.make_async_copy(
                                fin_src.at[g * half_bands + k],
                                fin_dst.at[micro],
                                fin_recv.at[micro],
                            ).start()

                        @pl.when(jnp.logical_not(here))
                        def _():
                            fin_copy(g, k).start()

    for m in range(batches):
        pltpu.make_async_copy(fin_src.at[0], fin_dst.at[m], fin_recv.at[m]).wait()
    out_ref[...] = fin_dst[...]

    for worker in range(workers):

        @pl.when(pix_sends(worker))
        def _():
            pix_copy(worker).wait_send()

    @pl.when(works & (seg < halfway))
    def _():
        mirror_copy.wait_send()

    @pl.when(works & (seg < last))
    def _():
        for copy in next_copies:
            copy.wait_send()

    @pl.when(works & (seg < halfway - 1))
    def _():
        for copy in skip_copies:
            copy.wait_send()

    @pl.when(works & (seg == last))
    def _():
        for g in range(segments):
            for k in range(half_bands):
                if g < last:
                    fin_copy(g, k).wait_send()
                else:

                    @pl.when(chunk_band(k) != band)
                    def _():
                        fin_copy(g, k).wait_send()


def shards(segments, bands, pixels, conv_weight, join_weight):
    batches, band_rows, columns, channels = pixels.shape
    layers = conv_weight.shape[1]
    own_rows = band_rows * bands // HALVES
    rows = own_rows + layers
    chunks = -(-rows // band_rows)
    own_px, halo_px, all_px = own_rows * columns, layers * columns, rows * columns
    share = columns // segments
    piece = band_rows * share
    block_rows = -(-piece // 16) * 16
    blocks = segments * (bands // HALVES)
    workers = HALVES * batches
    kept = jnp.bfloat16
    conv = conv_weight.reshape(layers, 3, 3 * channels, channels)
    join = join_weight.reshape(channels, channels)
    dma = pltpu.SemaphoreType.DMA
    result = pl.pallas_call(
        functools.partial(kernel, segments, bands),
        out_shape=jax.ShapeDtypeStruct((batches, block_rows, channels), kept),
        in_specs=[pl.BlockSpec(memory_space=pltpu.HBM)] * 3,
        out_specs=pl.BlockSpec(memory_space=pltpu.VMEM),
        scratch_shapes=[
            pltpu.VMEM((chunks, band_rows, columns, channels), kept),
            pltpu.VMEM((all_px, channels), kept),
            pltpu.VMEM((all_px, channels), kept),
            pltpu.VMEM((layers, 3, 3 * channels, channels), kept),
            pltpu.VMEM((channels, channels), kept),
            pltpu.VMEM((channels, channels), kept),
            pltpu.VMEM((all_px, channels), jnp.float32),
            pltpu.VMEM((all_px, channels), kept),
            pltpu.VMEM((all_px + columns, 3 * channels), kept),
            pltpu.VMEM((own_px, channels), kept),
            pltpu.VMEM((halo_px, channels), kept),
            pltpu.VMEM((blocks, block_rows, own_px), kept),
            pltpu.VMEM((blocks, block_rows, channels), kept),
            pltpu.VMEM((batches, block_rows, channels), kept),
            dma((layers, 3)),
            dma,
            dma((workers,)),
            dma((chunks,)),
            dma((2,)),
            dma((2,)),
            dma((2,)),
            dma((2,)),
            dma,
            dma,
            dma((blocks,)),
            dma((batches,)),
        ],
        compiler_params=pltpu.CompilerParams(collective_id=0, has_side_effects=True),
    )(pixels, conv, join)
    return result[:, :piece].reshape(batches, band_rows, share, channels)


def solution(mesh):
    return jax.shard_map(
        functools.partial(shards, mesh.shape["segment"], mesh.shape["band"]),
        mesh=mesh,
        in_specs=(
            P(None, "band", None, None),
            P("segment", None, None, None, None, None),
            P("segment", None, None),
        ),
        out_specs=P(None, "band", "segment", None),
        check_vma=False,
    )
```

```python
import functools

import jax
import jax.numpy as jnp
from jax import lax
from jax.experimental import pallas as pl
from jax.experimental.pallas import tpu as pltpu
from jax.sharding import PartitionSpec as P

MESH = pl.DeviceIdType.MESH
HALVES = 2


def unit(values):
    return values * lax.rsqrt(jnp.mean(values * values, axis=-1, keepdims=True) + 1e-05)


def kernel(
    segments,
    bands,
    pix_ref,
    conv_ref,
    join_ref,
    out_ref,
    pix_buf,
    in_buf,
    skip_buf,
    weight_buf,
    own_join,
    mirror_join,
    skip_part,
    hid,
    patches,
    own_out,
    halo_out,
    place,
    fin_src,
    fin_dst,
    weight_sem,
    join_sem,
    pix_send,
    pix_recv,
    in_send,
    in_recv,
    skip_send,
    skip_recv,
    mirror_send,
    mirror_recv,
    fin_send,
    fin_recv,
):
    batches, band_rows, columns, channels = pix_ref.shape
    layers = conv_ref.shape[0]
    workers = HALVES * batches
    chunks = pix_buf.shape[0]
    own_px = own_out.shape[0]
    halo_px = halo_out.shape[0]
    all_px = own_px + halo_px
    half_bands = bands // HALVES
    halfway = segments // 2
    last = segments - 1
    share = columns // segments
    seg = lax.axis_index("segment")
    band = lax.axis_index("band")
    lower = lax.rem(band, HALVES)
    micro = lax.div(band, HALVES)
    other = band + 1 - 2 * lower
    works = band < workers
    own_half = lax.div(band, half_bands)

    weight_copies = []
    for layer in range(layers):
        for dy in range(3):
            to = dy + lower * (2 - 2 * dy)
            weight_copies.append(
                pltpu.make_async_copy(
                    conv_ref.at[layer, dy], weight_buf.at[layer, to], weight_sem.at[layer, dy]
                )
            )
    join_copy = pltpu.make_async_copy(join_ref, own_join, join_sem)

    @pl.when(works)
    def _():
        for copy in weight_copies:
            copy.start()
        join_copy.start()

    barrier = pltpu.get_barrier_semaphore()

    def greet(to_seg, to_band):
        pl.semaphore_signal(barrier, inc=1, device_id=(to_seg, to_band), device_id_type=MESH)

    def chunk_band(chunk):
        return chunk + lower * (bands - 1 - 2 * chunk)

    @pl.when(works & (seg == 0))
    def _():
        for chunk in range(chunks):

            @pl.when(chunk_band(chunk) != band)
            def _():
                greet(0, chunk_band(chunk))

    @pl.when(works & (seg > 0))
    def _():
        greet(seg - 1, band)
        greet(seg - 1, other)

    @pl.when(works & (seg > halfway))
    def _():
        greet(last - seg, band)
        greet(last - seg, other)

    for m in range(batches):

        @pl.when((seg != last) | (band != HALVES * m + own_half))
        def _():
            greet(last, HALVES * m + own_half)

    def one_if(condition):
        return jnp.where(condition, 1, 0).astype(jnp.int32)

    def pix_chunk(worker):
        return band if worker % HALVES == 0 else bands - 1 - band

    def pix_sends(worker):
        return (seg == 0) & (pix_chunk(worker) < chunks) & (band != worker)

    expected = one_if(works & (seg < last)) * 2 + one_if(works & (seg < halfway - 1)) * 2
    for worker in range(workers):
        expected += one_if(pix_sends(worker))
    expected += one_if(works & (seg == last)) * (
        segments * half_bands - one_if(own_half == lower)
    )

    @pl.when(expected > 0)
    def _():
        pl.semaphore_wait(barrier, expected)

    def pix_copy(worker):
        return pltpu.make_async_remote_copy(
            src_ref=pix_ref.at[worker // HALVES],
            dst_ref=pix_buf.at[pix_chunk(worker)],
            send_sem=pix_send.at[worker],
            recv_sem=pix_recv.at[pix_chunk(worker)],
            device_id=(0, worker),
            device_id_type=MESH,
        )

    own_chunk = band + lower * (bands - 1 - 2 * band)
    for worker in range(workers):

        @pl.when(pix_sends(worker))
        def _():
            pix_copy(worker).start()

    @pl.when(works & (seg == 0) & (own_chunk < chunks))
    def _():
        pltpu.make_async_copy(
            pix_ref.at[micro], pix_buf.at[own_chunk], pix_recv.at[own_chunk]
        ).start()

    mirror_copy = pltpu.make_async_remote_copy(
        src_ref=join_ref,
        dst_ref=mirror_join,
        send_sem=mirror_send,
        recv_sem=mirror_recv,
        device_id=(last - seg, band),
        device_id_type=MESH,
    )

    @pl.when(works & (seg < halfway))
    def _():
        mirror_copy.start()

    def hop_copies(buffer, to_seg, send, recv):
        return (
            pltpu.make_async_remote_copy(
                src_ref=own_out,
                dst_ref=buffer.at[pl.ds(0, own_px)],
                send_sem=send.at[0],
                recv_sem=recv.at[0],
                device_id=(to_seg, band),
                device_id_type=MESH,
            ),
            pltpu.make_async_remote_copy(
                src_ref=halo_out,
                dst_ref=buffer.at[pl.ds(own_px, halo_px)],
                send_sem=send.at[1],
                recv_sem=recv.at[1],
                device_id=(to_seg, other),
                device_id_type=MESH,
            ),
        )

    next_copies = hop_copies(in_buf, seg + 1, in_send, in_recv)
    skip_copies = hop_copies(skip_buf, last - seg, skip_send, skip_recv)

    def fin_copy(g, k):
        return pltpu.make_async_remote_copy(
            src_ref=fin_src.at[g * half_bands + k],
            dst_ref=fin_dst.at[micro],
            send_sem=fin_send.at[g * half_bands + k],
            recv_sem=fin_recv.at[micro],
            device_id=(g, chunk_band(k)),
            device_id_type=MESH,
        )

    def dot(a, b):
        return jnp.dot(a, b, preferred_element_type=jnp.float32)

    @pl.when(works)
    def _():
        @pl.when(seg == last)
        def _():
            block_rows = fin_src.shape[1]
            at = lax.broadcasted_iota(jnp.int32, (block_rows, own_px), 0)
            pixel = lax.broadcasted_iota(jnp.int32, (block_rows, own_px), 1)
            row = jnp.zeros_like(at)
            for step in range(1, band_rows):
                row += jnp.where(at >= step * share, 1, 0)
            column = at - row * share
            row = row + lower * (band_rows - 1 - 2 * row)
            inside = at < band_rows * share
            base = row * columns + column
            for g in range(segments):
                for k in range(half_bands):
                    wanted = base + (k * band_rows * columns + g * share)
                    place[g * half_bands + k] = jnp.where(
                        inside & (pixel == wanted), 1.0, 0.0
                    ).astype(jnp.bfloat16)

        hid[...] = jnp.zeros_like(hid)
        span = 3 * channels
        patches[pl.ds(0, columns), pl.ds(0, span)] = jnp.zeros((columns, span), jnp.bfloat16)
        join_copy.wait()

        @pl.when(seg > 0)
        def _():
            for copy in weight_copies:
                copy.wait()

        @pl.when(seg >= halfway)
        def _():
            mirror_copy.wait_recv()

        @pl.when(seg > halfway)
        def _():
            for copy in skip_copies:
                copy.wait_recv()
            skip_part[...] = dot(skip_buf[...], mirror_join[...])

        def take_input():
            @pl.when(seg == 0)
            def _():
                for chunk in range(chunks):
                    pltpu.make_async_copy(
                        pix_ref.at[0], pix_buf.at[chunk], pix_recv.at[chunk]
                    ).wait()
                for row in range(all_px // columns):
                    within = row % band_rows
                    within = within + lower * (band_rows - 1 - 2 * within)
                    hid[pl.ds(row * columns, columns)] = pix_buf[row // band_rows, within]

            @pl.when(seg > 0)
            def _():
                for copy in next_copies:
                    copy.wait_recv()

            @pl.when((seg > 0) & (seg < halfway))
            def _():
                hid[...] = in_buf[...]

            @pl.when(seg == halfway)
            def _():
                skip_part[...] = dot(in_buf[...], mirror_join[...])

            @pl.when(seg >= halfway)
            def _():
                hid[...] = (skip_part[...] + dot(in_buf[...], own_join[...])).astype(jnp.bfloat16)

        keep = all_px - columns
        at = lax.broadcasted_iota(jnp.int32, (all_px // columns, columns, channels), 1).reshape(
            all_px, channels
        )

        def step(index, carry):
            @pl.when(index == 1)
            def _():
                take_input()

            layer = jnp.maximum(index - 1, 0)

            @pl.when(seg == 0)
            def _():
                for dy in range(3):
                    pltpu.make_async_copy(
                        conv_ref.at[layer, dy], weight_buf.at[layer, dy], weight_sem.at[layer, dy]
                    ).wait()

            scaled = unit(hid[...].astype(jnp.float32))
            left = jnp.where(at == 0, 0.0, pltpu.roll(scaled, 1, 0))
            right = jnp.where(at == columns - 1, 0.0, pltpu.roll(scaled, all_px - 1, 0))
            for dx, part in enumerate((left, scaled, right)):
                part = part.astype(jnp.bfloat16)
                patches[pl.ds(columns, keep - columns), pl.ds(dx * channels, channels)] = part[
                    : keep - columns
                ]
                patches[:, pl.ds(span + dx * channels, channels)] = part[:keep]
                patches[:, pl.ds(2 * span + dx * channels, channels)] = part[columns:]
            total = dot(patches[...], weight_buf[layer].reshape(3 * span, channels))
            hid[pl.ds(0, keep)] = (
                hid[pl.ds(0, keep)].astype(jnp.float32) + jnp.maximum(total, 0.0)
            ).astype(jnp.bfloat16)
            return carry

        lax.fori_loop(one_if(seg == 0), layers + 1, step, 0)
        hidden = hid[pl.ds(0, own_px)]

        @pl.when(seg < last)
        def _():
            for row in range(halo_px // columns):
                start = own_px - (row + 1) * columns
                halo_out[pl.ds(row * columns, columns)] = hidden[start : start + columns]
            own_out[...] = hidden
            for copy in next_copies[::-1]:
                copy.start()

            @pl.when(seg < halfway - 1)
            def _():
                for copy in skip_copies:
                    copy.start()

        @pl.when(seg == last)
        def _():
            decoded = unit(hidden.astype(jnp.float32)).astype(jnp.bfloat16)
            sorting = place[...].reshape(-1, own_px)
            fin_src[...] = dot(sorting, decoded).astype(jnp.bfloat16).reshape(fin_src.shape)
            for g in range(segments):
                for k in range(half_bands):
                    if g < last:
                        fin_copy(g, k).start()
                    else:
                        here = chunk_band(k) == band

                        @pl.when(here)
                        def _():
                            pltpu.make_async_copy(
                                fin_src.at[g * half_bands + k],
                                fin_dst.at[micro],
                                fin_recv.at[micro],
                            ).start()

                        @pl.when(jnp.logical_not(here))
                        def _():
                            fin_copy(g, k).start()

    for m in range(batches):
        pltpu.make_async_copy(fin_src.at[0], fin_dst.at[m], fin_recv.at[m]).wait()
    out_ref[...] = fin_dst[:, : out_ref.shape[1]]

    for worker in range(workers):

        @pl.when(pix_sends(worker))
        def _():
            pix_copy(worker).wait_send()

    @pl.when(works & (seg < halfway))
    def _():
        mirror_copy.wait_send()

    @pl.when(works & (seg < last))
    def _():
        for copy in next_copies:
            copy.wait_send()

    @pl.when(works & (seg < halfway - 1))
    def _():
        for copy in skip_copies:
            copy.wait_send()

    @pl.when(works & (seg == last))
    def _():
        for g in range(segments):
            for k in range(half_bands):
                if g < last:
                    fin_copy(g, k).wait_send()
                else:

                    @pl.when(chunk_band(k) != band)
                    def _():
                        fin_copy(g, k).wait_send()


def shards(segments, bands, pixels, conv_weight, join_weight):
    batches, band_rows, columns, channels = pixels.shape
    layers = conv_weight.shape[1]
    own_rows = band_rows * bands // HALVES
    rows = own_rows + layers
    chunks = -(-rows // band_rows)
    own_px, halo_px, all_px = own_rows * columns, layers * columns, rows * columns
    share = columns // segments
    piece = band_rows * share
    block_rows = -(-piece // 16) * 16
    blocks = segments * (bands // HALVES)
    workers = HALVES * batches
    kept = jnp.bfloat16
    conv = conv_weight.reshape(layers, 3, 3 * channels, channels)
    join = join_weight.reshape(channels, channels)
    dma = pltpu.SemaphoreType.DMA
    result = pl.pallas_call(
        functools.partial(kernel, segments, bands),
        out_shape=jax.ShapeDtypeStruct((batches, piece, channels), kept),
        in_specs=[pl.BlockSpec(memory_space=pltpu.HBM)] * 3,
        out_specs=pl.BlockSpec(memory_space=pltpu.VMEM),
        scratch_shapes=[
            pltpu.VMEM((chunks, band_rows, columns, channels), kept),
            pltpu.VMEM((all_px, channels), kept),
            pltpu.VMEM((all_px, channels), kept),
            pltpu.VMEM((layers, 3, 3 * channels, channels), kept),
            pltpu.VMEM((channels, channels), kept),
            pltpu.VMEM((channels, channels), kept),
            pltpu.VMEM((all_px, channels), jnp.float32),
            pltpu.VMEM((all_px, channels), kept),
            pltpu.VMEM((all_px - columns, 9 * channels), kept),
            pltpu.VMEM((own_px, channels), kept),
            pltpu.VMEM((halo_px, channels), kept),
            pltpu.VMEM((blocks, block_rows, own_px), kept),
            pltpu.VMEM((blocks, block_rows, channels), kept),
            pltpu.VMEM((batches, block_rows, channels), kept),
            dma((layers, 3)),
            dma,
            dma((workers,)),
            dma((chunks,)),
            dma((2,)),
            dma((2,)),
            dma((2,)),
            dma((2,)),
            dma,
            dma,
            dma((blocks,)),
            dma((batches,)),
        ],
        compiler_params=pltpu.CompilerParams(collective_id=0, has_side_effects=True),
    )(pixels, conv, join)
    return result.reshape(batches, band_rows, share, channels)


def solution(mesh):
    return jax.shard_map(
        functools.partial(shards, mesh.shape["segment"], mesh.shape["band"]),
        mesh=mesh,
        in_specs=(
            P(None, "band", None, None),
            P("segment", None, None, None, None, None),
            P("segment", None, None),
        ),
        out_specs=P(None, "band", "segment", None),
        check_vma=False,
    )
```

```python
import functools

import jax
import jax.numpy as jnp
from jax import lax
from jax.experimental import pallas as pl
from jax.experimental.pallas import tpu as pltpu
from jax.sharding import PartitionSpec as P

MESH = pl.DeviceIdType.MESH
HALVES = 2


def unit(values):
    return values * lax.rsqrt(jnp.mean(values * values, axis=-1, keepdims=True) + 1e-05)


def kernel(
    segments,
    bands,
    pix_ref,
    conv_ref,
    join_ref,
    out_ref,
    pix_buf,
    in_buf,
    skip_buf,
    weight_buf,
    own_join,
    mirror_join,
    skip_part,
    hid,
    wide,
    own_out,
    halo_out,
    place,
    fin_src,
    fin_dst,
    weight_sem,
    join_sem,
    pix_send,
    pix_recv,
    in_send,
    in_recv,
    skip_send,
    skip_recv,
    mirror_send,
    mirror_recv,
    fin_send,
    fin_recv,
):
    batches, band_rows, columns, channels = pix_ref.shape
    layers = conv_ref.shape[0]
    workers = HALVES * batches
    chunks = pix_buf.shape[0]
    own_px = own_out.shape[0]
    halo_px = halo_out.shape[0]
    all_px = own_px + halo_px
    half_bands = bands // HALVES
    halfway = segments // 2
    last = segments - 1
    share = columns // segments
    seg = lax.axis_index("segment")
    band = lax.axis_index("band")
    lower = lax.rem(band, HALVES)
    micro = lax.div(band, HALVES)
    other = band + 1 - 2 * lower
    works = band < workers
    own_half = lax.div(band, half_bands)

    weight_copies = []
    for layer in range(layers):
        for dy in range(3):
            to = dy + lower * (2 - 2 * dy)
            weight_copies.append(
                pltpu.make_async_copy(
                    conv_ref.at[layer, dy], weight_buf.at[layer, to], weight_sem.at[layer, dy]
                )
            )
    join_copy = pltpu.make_async_copy(join_ref, own_join, join_sem)

    @pl.when(works)
    def _():
        for copy in weight_copies:
            copy.start()
        join_copy.start()

    barrier = pltpu.get_barrier_semaphore()

    def greet(to_seg, to_band):
        pl.semaphore_signal(barrier, inc=1, device_id=(to_seg, to_band), device_id_type=MESH)

    def chunk_band(chunk):
        return chunk + lower * (bands - 1 - 2 * chunk)

    @pl.when(works & (seg == 0))
    def _():
        for chunk in range(chunks):

            @pl.when(chunk_band(chunk) != band)
            def _():
                greet(0, chunk_band(chunk))

    @pl.when(works & (seg > 0))
    def _():
        greet(seg - 1, band)
        greet(seg - 1, other)

    @pl.when(works & (seg > halfway))
    def _():
        greet(last - seg, band)
        greet(last - seg, other)

    for m in range(batches):

        @pl.when((seg != last) | (band != HALVES * m + own_half))
        def _():
            greet(last, HALVES * m + own_half)

    def one_if(condition):
        return jnp.where(condition, 1, 0).astype(jnp.int32)

    def pix_chunk(worker):
        return band if worker % HALVES == 0 else bands - 1 - band

    def pix_sends(worker):
        return (seg == 0) & (pix_chunk(worker) < chunks) & (band != worker)

    expected = one_if(works & (seg < last)) * 2 + one_if(works & (seg < halfway - 1)) * 2
    for worker in range(workers):
        expected += one_if(pix_sends(worker))
    expected += one_if(works & (seg == last)) * (
        segments * half_bands - one_if(own_half == lower)
    )

    @pl.when(expected > 0)
    def _():
        pl.semaphore_wait(barrier, expected)

    def pix_copy(worker):
        return pltpu.make_async_remote_copy(
            src_ref=pix_ref.at[worker // HALVES],
            dst_ref=pix_buf.at[pix_chunk(worker)],
            send_sem=pix_send.at[worker],
            recv_sem=pix_recv.at[pix_chunk(worker)],
            device_id=(0, worker),
            device_id_type=MESH,
        )

    own_chunk = band + lower * (bands - 1 - 2 * band)
    for worker in range(workers):

        @pl.when(pix_sends(worker))
        def _():
            pix_copy(worker).start()

    @pl.when(works & (seg == 0) & (own_chunk < chunks))
    def _():
        pltpu.make_async_copy(
            pix_ref.at[micro], pix_buf.at[own_chunk], pix_recv.at[own_chunk]
        ).start()

    mirror_copy = pltpu.make_async_remote_copy(
        src_ref=join_ref,
        dst_ref=mirror_join,
        send_sem=mirror_send,
        recv_sem=mirror_recv,
        device_id=(last - seg, band),
        device_id_type=MESH,
    )

    @pl.when(works & (seg < halfway))
    def _():
        mirror_copy.start()

    def hop_copies(buffer, to_seg, send, recv):
        return (
            pltpu.make_async_remote_copy(
                src_ref=own_out,
                dst_ref=buffer.at[pl.ds(0, own_px)],
                send_sem=send.at[0],
                recv_sem=recv.at[0],
                device_id=(to_seg, band),
                device_id_type=MESH,
            ),
            pltpu.make_async_remote_copy(
                src_ref=halo_out,
                dst_ref=buffer.at[pl.ds(own_px, halo_px)],
                send_sem=send.at[1],
                recv_sem=recv.at[1],
                device_id=(to_seg, other),
                device_id_type=MESH,
            ),
        )

    next_copies = hop_copies(in_buf, seg + 1, in_send, in_recv)
    skip_copies = hop_copies(skip_buf, last - seg, skip_send, skip_recv)

    def fin_copy(g, k):
        return pltpu.make_async_remote_copy(
            src_ref=fin_src.at[g * half_bands + k],
            dst_ref=fin_dst.at[micro],
            send_sem=fin_send.at[g * half_bands + k],
            recv_sem=fin_recv.at[micro],
            device_id=(g, chunk_band(k)),
            device_id_type=MESH,
        )

    def dot(a, b):
        return jnp.dot(a, b, preferred_element_type=jnp.float32)

    @pl.when(works)
    def _():
        @pl.when(seg == last)
        def _():
            block_rows = fin_src.shape[1]
            at = lax.broadcasted_iota(jnp.int32, (block_rows, own_px), 0)
            pixel = lax.broadcasted_iota(jnp.int32, (block_rows, own_px), 1)
            row = jnp.zeros_like(at)
            for step in range(1, band_rows):
                row += jnp.where(at >= step * share, 1, 0)
            column = at - row * share
            row = row + lower * (band_rows - 1 - 2 * row)
            inside = at < band_rows * share
            base = row * columns + column
            for g in range(segments):
                for k in range(half_bands):
                    wanted = base + (k * band_rows * columns + g * share)
                    place[g * half_bands + k] = jnp.where(
                        inside & (pixel == wanted), 1.0, 0.0
                    ).astype(jnp.bfloat16)

        hid[...] = jnp.zeros_like(hid)
        span = 3 * channels
        wide[pl.ds(0, columns)] = jnp.zeros((columns, span), jnp.bfloat16)
        join_copy.wait()

        @pl.when(seg > 0)
        def _():
            for copy in weight_copies:
                copy.wait()

        @pl.when(seg >= halfway)
        def _():
            mirror_copy.wait_recv()

        @pl.when(seg > halfway)
        def _():
            for copy in skip_copies:
                copy.wait_recv()
            skip_part[...] = dot(skip_buf[...], mirror_join[...])

        def take_input():
            @pl.when(seg == 0)
            def _():
                for chunk in range(chunks):
                    pltpu.make_async_copy(
                        pix_ref.at[0], pix_buf.at[chunk], pix_recv.at[chunk]
                    ).wait()
                for row in range(all_px // columns):
                    within = row % band_rows
                    within = within + lower * (band_rows - 1 - 2 * within)
                    hid[pl.ds(row * columns, columns)] = pix_buf[row // band_rows, within]

            @pl.when(seg > 0)
            def _():
                for copy in next_copies:
                    copy.wait_recv()

            @pl.when((seg > 0) & (seg < halfway))
            def _():
                hid[...] = in_buf[...]

            @pl.when(seg == halfway)
            def _():
                skip_part[...] = dot(in_buf[...], mirror_join[...])

            @pl.when(seg >= halfway)
            def _():
                hid[...] = (skip_part[...] + dot(in_buf[...], own_join[...])).astype(jnp.bfloat16)

        keep = all_px - columns
        at = lax.broadcasted_iota(jnp.int32, (all_px // columns, columns, channels), 1).reshape(
            all_px, channels
        )

        first = -(-keep // (2 * columns)) * columns
        blocks = ((0, first), (first, keep - first))

        def step(index, carry):
            @pl.when(index == 1)
            def _():
                take_input()

            layer = jnp.maximum(index - 1, 0)

            @pl.when(seg == 0)
            def _():
                for dy in range(3):
                    pltpu.make_async_copy(
                        conv_ref.at[layer, dy], weight_buf.at[layer, dy], weight_sem.at[layer, dy]
                    ).wait()

            scaled = unit(hid[...].astype(jnp.float32))
            left = jnp.where(at == 0, 0.0, pltpu.roll(scaled, 1, 0))
            right = jnp.where(at == columns - 1, 0.0, pltpu.roll(scaled, all_px - 1, 0))
            for dx, part in enumerate((left, scaled, right)):
                wide[pl.ds(columns, all_px), pl.ds(dx * channels, channels)] = part.astype(
                    jnp.bfloat16
                )
            for start, size in blocks:
                total = dot(wide[pl.ds(start, size)], weight_buf[layer, 0])
                for dy in range(1, 3):
                    total += dot(wide[pl.ds(start + dy * columns, size)], weight_buf[layer, dy])
                hid[pl.ds(start, size)] = (
                    hid[pl.ds(start, size)].astype(jnp.float32) + jnp.maximum(total, 0.0)
                ).astype(jnp.bfloat16)
            return carry

        lax.fori_loop(one_if(seg == 0), layers + 1, step, 0)
        hidden = hid[pl.ds(0, own_px)]

        @pl.when(seg < last)
        def _():
            for row in range(halo_px // columns):
                start = own_px - (row + 1) * columns
                halo_out[pl.ds(row * columns, columns)] = hidden[start : start + columns]
            own_out[...] = hidden
            for copy in next_copies[::-1]:
                copy.start()

            @pl.when(seg < halfway - 1)
            def _():
                for copy in skip_copies:
                    copy.start()

        @pl.when(seg == last)
        def _():
            decoded = unit(hidden.astype(jnp.float32)).astype(jnp.bfloat16)
            sorting = place[...].reshape(-1, own_px)
            fin_src[...] = dot(sorting, decoded).astype(jnp.bfloat16).reshape(fin_src.shape)
            for g in range(segments):
                for k in range(half_bands):
                    if g < last:
                        fin_copy(g, k).start()
                    else:
                        here = chunk_band(k) == band

                        @pl.when(here)
                        def _():
                            pltpu.make_async_copy(
                                fin_src.at[g * half_bands + k],
                                fin_dst.at[micro],
                                fin_recv.at[micro],
                            ).start()

                        @pl.when(jnp.logical_not(here))
                        def _():
                            fin_copy(g, k).start()

    for m in range(batches):
        pltpu.make_async_copy(fin_src.at[0], fin_dst.at[m], fin_recv.at[m]).wait()
    out_ref[...] = fin_dst[:, : out_ref.shape[1]]

    for worker in range(workers):

        @pl.when(pix_sends(worker))
        def _():
            pix_copy(worker).wait_send()

    @pl.when(works & (seg < halfway))
    def _():
        mirror_copy.wait_send()

    @pl.when(works & (seg < last))
    def _():
        for copy in next_copies:
            copy.wait_send()

    @pl.when(works & (seg < halfway - 1))
    def _():
        for copy in skip_copies:
            copy.wait_send()

    @pl.when(works & (seg == last))
    def _():
        for g in range(segments):
            for k in range(half_bands):
                if g < last:
                    fin_copy(g, k).wait_send()
                else:

                    @pl.when(chunk_band(k) != band)
                    def _():
                        fin_copy(g, k).wait_send()


def shards(segments, bands, pixels, conv_weight, join_weight):
    batches, band_rows, columns, channels = pixels.shape
    layers = conv_weight.shape[1]
    own_rows = band_rows * bands // HALVES
    rows = own_rows + layers
    chunks = -(-rows // band_rows)
    own_px, halo_px, all_px = own_rows * columns, layers * columns, rows * columns
    share = columns // segments
    piece = band_rows * share
    block_rows = -(-piece // 16) * 16
    blocks = segments * (bands // HALVES)
    workers = HALVES * batches
    kept = jnp.bfloat16
    conv = conv_weight.reshape(layers, 3, 3 * channels, channels)
    join = join_weight.reshape(channels, channels)
    dma = pltpu.SemaphoreType.DMA
    result = pl.pallas_call(
        functools.partial(kernel, segments, bands),
        out_shape=jax.ShapeDtypeStruct((batches, piece, channels), kept),
        in_specs=[pl.BlockSpec(memory_space=pltpu.HBM)] * 3,
        out_specs=pl.BlockSpec(memory_space=pltpu.VMEM),
        scratch_shapes=[
            pltpu.VMEM((chunks, band_rows, columns, channels), kept),
            pltpu.VMEM((all_px, channels), kept),
            pltpu.VMEM((all_px, channels), kept),
            pltpu.VMEM((layers, 3, 3 * channels, channels), kept),
            pltpu.VMEM((channels, channels), kept),
            pltpu.VMEM((channels, channels), kept),
            pltpu.VMEM((all_px, channels), jnp.float32),
            pltpu.VMEM((all_px, channels), kept),
            pltpu.VMEM((all_px + columns, 3 * channels), kept),
            pltpu.VMEM((own_px, channels), kept),
            pltpu.VMEM((halo_px, channels), kept),
            pltpu.VMEM((blocks, block_rows, own_px), kept),
            pltpu.VMEM((blocks, block_rows, channels), kept),
            pltpu.VMEM((batches, block_rows, channels), kept),
            dma((layers, 3)),
            dma,
            dma((workers,)),
            dma((chunks,)),
            dma((2,)),
            dma((2,)),
            dma((2,)),
            dma((2,)),
            dma,
            dma,
            dma((blocks,)),
            dma((batches,)),
        ],
        compiler_params=pltpu.CompilerParams(collective_id=0, has_side_effects=True),
    )(pixels, conv, join)
    return result.reshape(batches, band_rows, share, channels)


def solution(mesh):
    return jax.shard_map(
        functools.partial(shards, mesh.shape["segment"], mesh.shape["band"]),
        mesh=mesh,
        in_specs=(
            P(None, "band", None, None),
            P("segment", None, None, None, None, None),
            P("segment", None, None),
        ),
        out_specs=P(None, "band", "segment", None),
        check_vma=False,
    )
```

```python
import functools

import jax
import jax.numpy as jnp
from jax import lax
from jax.experimental import pallas as pl
from jax.experimental.pallas import tpu as pltpu
from jax.sharding import PartitionSpec as P

MESH = pl.DeviceIdType.MESH
HALVES = 2


def unit(values):
    return values * lax.rsqrt(jnp.mean(values * values, axis=-1, keepdims=True) + 1e-05)


def kernel(
    segments,
    bands,
    pix_ref,
    conv_ref,
    join_ref,
    out_ref,
    pix_buf,
    in_buf,
    skip_buf,
    weight_buf,
    own_join,
    mirror_join,
    skip_part,
    hid,
    wide,
    own_out,
    halo_out,
    place,
    fin_src,
    fin_dst,
    weight_sem,
    join_sem,
    pix_send,
    pix_recv,
    in_send,
    in_recv,
    skip_send,
    skip_recv,
    mirror_send,
    mirror_recv,
    fin_send,
    fin_recv,
):
    batches, band_rows, columns, channels = pix_ref.shape
    layers = conv_ref.shape[0]
    workers = HALVES * batches
    chunks = pix_buf.shape[0]
    own_px = own_out.shape[0]
    halo_px = halo_out.shape[0]
    all_px = own_px + halo_px
    half_bands = bands // HALVES
    halfway = segments // 2
    last = segments - 1
    share = columns // segments
    seg = lax.axis_index("segment")
    band = lax.axis_index("band")
    lower = lax.rem(band, HALVES)
    micro = lax.div(band, HALVES)
    other = band + 1 - 2 * lower
    works = band < workers
    own_half = lax.div(band, half_bands)

    weight_copies = []
    for layer in range(layers):
        for dy in range(3):
            to = dy + lower * (2 - 2 * dy)
            weight_copies.append(
                pltpu.make_async_copy(
                    conv_ref.at[layer, dy], weight_buf.at[layer, to], weight_sem.at[layer, dy]
                )
            )
    join_copy = pltpu.make_async_copy(join_ref, own_join, join_sem)

    @pl.when(works)
    def _():
        for copy in weight_copies:
            copy.start()
        join_copy.start()

    barrier = pltpu.get_barrier_semaphore()

    def greet(to_seg, to_band):
        pl.semaphore_signal(barrier, inc=1, device_id=(to_seg, to_band), device_id_type=MESH)

    def chunk_band(chunk):
        return chunk + lower * (bands - 1 - 2 * chunk)

    @pl.when(works & (seg == 0))
    def _():
        for chunk in range(chunks):

            @pl.when(chunk_band(chunk) != band)
            def _():
                greet(0, chunk_band(chunk))

    @pl.when(works & (seg > 0))
    def _():
        greet(seg - 1, band)
        greet(seg - 1, other)

    @pl.when(works & (seg > halfway))
    def _():
        greet(last - seg, band)
        greet(last - seg, other)

    for m in range(batches):

        @pl.when((seg != last) | (band != HALVES * m + own_half))
        def _():
            greet(last, HALVES * m + own_half)

    def one_if(condition):
        return jnp.where(condition, 1, 0).astype(jnp.int32)

    def pix_chunk(worker):
        return band if worker % HALVES == 0 else bands - 1 - band

    def pix_sends(worker):
        return (seg == 0) & (pix_chunk(worker) < chunks) & (band != worker)

    expected = one_if(works & (seg < last)) * 2 + one_if(works & (seg < halfway - 1)) * 2
    for worker in range(workers):
        expected += one_if(pix_sends(worker))
    expected += one_if(works & (seg == last)) * (
        segments * half_bands - one_if(own_half == lower)
    )

    @pl.when(expected > 0)
    def _():
        pl.semaphore_wait(barrier, expected)

    def pix_copy(worker):
        return pltpu.make_async_remote_copy(
            src_ref=pix_ref.at[worker // HALVES],
            dst_ref=pix_buf.at[pix_chunk(worker)],
            send_sem=pix_send.at[worker],
            recv_sem=pix_recv.at[pix_chunk(worker)],
            device_id=(0, worker),
            device_id_type=MESH,
        )

    own_chunk = band + lower * (bands - 1 - 2 * band)
    for worker in range(workers):

        @pl.when(pix_sends(worker))
        def _():
            pix_copy(worker).start()

    @pl.when(works & (seg == 0) & (own_chunk < chunks))
    def _():
        pltpu.make_async_copy(
            pix_ref.at[micro], pix_buf.at[own_chunk], pix_recv.at[own_chunk]
        ).start()

    mirror_copy = pltpu.make_async_remote_copy(
        src_ref=join_ref,
        dst_ref=mirror_join,
        send_sem=mirror_send,
        recv_sem=mirror_recv,
        device_id=(last - seg, band),
        device_id_type=MESH,
    )

    @pl.when(works & (seg < halfway))
    def _():
        mirror_copy.start()

    def hop_copies(buffer, to_seg, send, recv):
        return (
            pltpu.make_async_remote_copy(
                src_ref=own_out,
                dst_ref=buffer.at[pl.ds(0, own_px)],
                send_sem=send.at[0],
                recv_sem=recv.at[0],
                device_id=(to_seg, band),
                device_id_type=MESH,
            ),
            pltpu.make_async_remote_copy(
                src_ref=halo_out,
                dst_ref=buffer.at[pl.ds(own_px, halo_px)],
                send_sem=send.at[1],
                recv_sem=recv.at[1],
                device_id=(to_seg, other),
                device_id_type=MESH,
            ),
        )

    next_copies = hop_copies(in_buf, seg + 1, in_send, in_recv)
    skip_copies = hop_copies(skip_buf, last - seg, skip_send, skip_recv)

    def fin_copy(g, k):
        return pltpu.make_async_remote_copy(
            src_ref=fin_src.at[g * half_bands + k],
            dst_ref=fin_dst.at[micro],
            send_sem=fin_send.at[g * half_bands + k],
            recv_sem=fin_recv.at[micro],
            device_id=(g, chunk_band(k)),
            device_id_type=MESH,
        )

    def dot(a, b):
        return jnp.dot(a, b, preferred_element_type=jnp.float32)

    @pl.when(works)
    def _():
        @pl.when(seg == last)
        def _():
            block_rows = fin_src.shape[1]
            at = lax.broadcasted_iota(jnp.int32, (block_rows, own_px), 0)
            pixel = lax.broadcasted_iota(jnp.int32, (block_rows, own_px), 1)
            row = jnp.zeros_like(at)
            for step in range(1, band_rows):
                row += jnp.where(at >= step * share, 1, 0)
            column = at - row * share
            row = row + lower * (band_rows - 1 - 2 * row)
            inside = at < band_rows * share
            base = row * columns + column
            for g in range(segments):
                for k in range(half_bands):
                    wanted = base + (k * band_rows * columns + g * share)
                    place[g * half_bands + k] = jnp.where(
                        inside & (pixel == wanted), 1.0, 0.0
                    ).astype(jnp.bfloat16)

        hid[...] = jnp.zeros_like(hid)
        wide[:, pl.ds(0, columns)] = jnp.zeros((3, columns, channels), jnp.bfloat16)
        join_copy.wait()

        @pl.when(seg > 0)
        def _():
            for copy in weight_copies:
                copy.wait()

        @pl.when(seg >= halfway)
        def _():
            mirror_copy.wait_recv()

        @pl.when(seg > halfway)
        def _():
            for copy in skip_copies:
                copy.wait_recv()
            skip_part[...] = dot(skip_buf[...], mirror_join[...])

        def take_input():
            @pl.when(seg == 0)
            def _():
                for chunk in range(chunks):
                    pltpu.make_async_copy(
                        pix_ref.at[0], pix_buf.at[chunk], pix_recv.at[chunk]
                    ).wait()
                for row in range(all_px // columns):
                    within = row % band_rows
                    within = within + lower * (band_rows - 1 - 2 * within)
                    hid[pl.ds(row * columns, columns)] = pix_buf[row // band_rows, within]

            @pl.when(seg > 0)
            def _():
                for copy in next_copies:
                    copy.wait_recv()

            @pl.when((seg > 0) & (seg < halfway))
            def _():
                hid[...] = in_buf[...]

            @pl.when(seg == halfway)
            def _():
                skip_part[...] = dot(in_buf[...], mirror_join[...])

            @pl.when(seg >= halfway)
            def _():
                hid[...] = (skip_part[...] + dot(in_buf[...], own_join[...])).astype(jnp.bfloat16)

        keep = all_px - columns
        at = lax.broadcasted_iota(jnp.int32, (all_px // columns, columns, channels), 1).reshape(
            all_px, channels
        )


        def step(index, carry):
            @pl.when(index == 1)
            def _():
                take_input()

            layer = jnp.maximum(index - 1, 0)

            @pl.when(seg == 0)
            def _():
                for dy in range(3):
                    pltpu.make_async_copy(
                        conv_ref.at[layer, dy], weight_buf.at[layer, dy], weight_sem.at[layer, dy]
                    ).wait()

            scaled = unit(hid[...].astype(jnp.float32))
            total = jnp.zeros((keep, channels), jnp.float32)
            for dx in (1, 0, 2):
                part = scaled
                if dx == 0:
                    part = jnp.where(at == 0, 0.0, pltpu.roll(scaled, 1, 0))
                if dx == 2:
                    part = jnp.where(at == columns - 1, 0.0, pltpu.roll(scaled, all_px - 1, 0))
                wide[dx, pl.ds(columns, all_px)] = part.astype(jnp.bfloat16)
                for dy in range(3):
                    total += dot(
                        wide[dx, pl.ds(dy * columns, keep)],
                        weight_buf[layer, dy, pl.ds(dx * channels, channels)],
                    )
            hid[pl.ds(0, keep)] = (
                hid[pl.ds(0, keep)].astype(jnp.float32) + jnp.maximum(total, 0.0)
            ).astype(jnp.bfloat16)
            return carry

        lax.fori_loop(one_if(seg == 0), layers + 1, step, 0)
        hidden = hid[pl.ds(0, own_px)]

        @pl.when(seg < last)
        def _():
            for row in range(halo_px // columns):
                start = own_px - (row + 1) * columns
                halo_out[pl.ds(row * columns, columns)] = hidden[start : start + columns]
            own_out[...] = hidden
            for copy in next_copies[::-1]:
                copy.start()

            @pl.when(seg < halfway - 1)
            def _():
                for copy in skip_copies:
                    copy.start()

        @pl.when(seg == last)
        def _():
            decoded = unit(hidden.astype(jnp.float32)).astype(jnp.bfloat16)
            sorting = place[...].reshape(-1, own_px)
            fin_src[...] = dot(sorting, decoded).astype(jnp.bfloat16).reshape(fin_src.shape)
            for g in range(segments):
                for k in range(half_bands):
                    if g < last:
                        fin_copy(g, k).start()
                    else:
                        here = chunk_band(k) == band

                        @pl.when(here)
                        def _():
                            pltpu.make_async_copy(
                                fin_src.at[g * half_bands + k],
                                fin_dst.at[micro],
                                fin_recv.at[micro],
                            ).start()

                        @pl.when(jnp.logical_not(here))
                        def _():
                            fin_copy(g, k).start()

    for m in range(batches):
        pltpu.make_async_copy(fin_src.at[0], fin_dst.at[m], fin_recv.at[m]).wait()
    out_ref[...] = fin_dst[:, : out_ref.shape[1]]

    for worker in range(workers):

        @pl.when(pix_sends(worker))
        def _():
            pix_copy(worker).wait_send()

    @pl.when(works & (seg < halfway))
    def _():
        mirror_copy.wait_send()

    @pl.when(works & (seg < last))
    def _():
        for copy in next_copies:
            copy.wait_send()

    @pl.when(works & (seg < halfway - 1))
    def _():
        for copy in skip_copies:
            copy.wait_send()

    @pl.when(works & (seg == last))
    def _():
        for g in range(segments):
            for k in range(half_bands):
                if g < last:
                    fin_copy(g, k).wait_send()
                else:

                    @pl.when(chunk_band(k) != band)
                    def _():
                        fin_copy(g, k).wait_send()


def shards(segments, bands, pixels, conv_weight, join_weight):
    batches, band_rows, columns, channels = pixels.shape
    layers = conv_weight.shape[1]
    own_rows = band_rows * bands // HALVES
    rows = own_rows + layers
    chunks = -(-rows // band_rows)
    own_px, halo_px, all_px = own_rows * columns, layers * columns, rows * columns
    share = columns // segments
    piece = band_rows * share
    block_rows = -(-piece // 16) * 16
    blocks = segments * (bands // HALVES)
    workers = HALVES * batches
    kept = jnp.bfloat16
    conv = conv_weight.reshape(layers, 3, 3 * channels, channels)
    join = join_weight.reshape(channels, channels)
    dma = pltpu.SemaphoreType.DMA
    result = pl.pallas_call(
        functools.partial(kernel, segments, bands),
        out_shape=jax.ShapeDtypeStruct((batches, piece, channels), kept),
        in_specs=[pl.BlockSpec(memory_space=pltpu.HBM)] * 3,
        out_specs=pl.BlockSpec(memory_space=pltpu.VMEM),
        scratch_shapes=[
            pltpu.VMEM((chunks, band_rows, columns, channels), kept),
            pltpu.VMEM((all_px, channels), kept),
            pltpu.VMEM((all_px, channels), kept),
            pltpu.VMEM((layers, 3, 3 * channels, channels), kept),
            pltpu.VMEM((channels, channels), kept),
            pltpu.VMEM((channels, channels), kept),
            pltpu.VMEM((all_px, channels), jnp.float32),
            pltpu.VMEM((all_px, channels), kept),
            pltpu.VMEM((3, all_px + columns, channels), kept),
            pltpu.VMEM((own_px, channels), kept),
            pltpu.VMEM((halo_px, channels), kept),
            pltpu.VMEM((blocks, block_rows, own_px), kept),
            pltpu.VMEM((blocks, block_rows, channels), kept),
            pltpu.VMEM((batches, block_rows, channels), kept),
            dma((layers, 3)),
            dma,
            dma((workers,)),
            dma((chunks,)),
            dma((2,)),
            dma((2,)),
            dma((2,)),
            dma((2,)),
            dma,
            dma,
            dma((blocks,)),
            dma((batches,)),
        ],
        compiler_params=pltpu.CompilerParams(collective_id=0, has_side_effects=True),
    )(pixels, conv, join)
    return result.reshape(batches, band_rows, share, channels)


def solution(mesh):
    return jax.shard_map(
        functools.partial(shards, mesh.shape["segment"], mesh.shape["band"]),
        mesh=mesh,
        in_specs=(
            P(None, "band", None, None),
            P("segment", None, None, None, None, None),
            P("segment", None, None),
        ),
        out_specs=P(None, "band", "segment", None),
        check_vma=False,
    )
```

```python
import functools

import jax
import jax.numpy as jnp
from jax import lax
from jax.experimental import pallas as pl
from jax.experimental.pallas import tpu as pltpu
from jax.sharding import PartitionSpec as P

MESH = pl.DeviceIdType.MESH
HALVES = 2


def unit(values):
    return values * lax.rsqrt(jnp.mean(values * values, axis=-1, keepdims=True) + 1e-05)


def kernel(
    segments,
    bands,
    pix_ref,
    conv_ref,
    join_ref,
    out_ref,
    pix_buf,
    in_buf,
    skip_buf,
    early_skip,
    early_out,
    weight_buf,
    own_join,
    mirror_join,
    skip_part,
    hid,
    wide,
    own_out,
    halo_out,
    place,
    fin_src,
    fin_dst,
    weight_sem,
    join_sem,
    pix_send,
    pix_recv,
    in_send,
    in_recv,
    skip_send,
    skip_recv,
    mirror_send,
    mirror_recv,
    feed_send,
    feed_recv,
    early_send,
    early_recv,
    fin_send,
    fin_recv,
):
    batches, band_rows, columns, channels = pix_ref.shape
    layers = conv_ref.shape[0]
    workers = HALVES * batches
    chunks = pix_buf.shape[0]
    own_px = own_out.shape[0]
    halo_px = halo_out.shape[0]
    all_px = own_px + halo_px
    half_bands = bands // HALVES
    halfway = segments // 2
    last = segments - 1
    tail = segments - 2
    share = columns // segments
    seg = lax.axis_index("segment")
    band = lax.axis_index("band")
    lower = lax.rem(band, HALVES)
    micro = lax.div(band, HALVES)
    other = band + 1 - 2 * lower
    works = (band < workers) & (lax.rem(seg, 2) == 0)
    feeds = (band < workers) & (lax.rem(seg, 2) == 1)
    own_half = lax.div(band, half_bands)

    weight_copies = []
    for layer in range(layers):
        for dy in range(3):
            to = dy + lower * (2 - 2 * dy)
            weight_copies.append(
                pltpu.make_async_copy(
                    conv_ref.at[layer, dy], weight_buf.at[layer, to], weight_sem.at[layer, dy]
                )
            )
    join_copy = pltpu.make_async_copy(join_ref, own_join.at[0], join_sem)

    @pl.when(works)
    def _():
        for copy in weight_copies:
            copy.start()
        join_copy.start()

    barrier = pltpu.get_barrier_semaphore()

    def greet(to_seg, to_band):
        pl.semaphore_signal(barrier, inc=1, device_id=(to_seg, to_band), device_id_type=MESH)

    def chunk_band(chunk):
        return chunk + lower * (bands - 1 - 2 * chunk)

    @pl.when(works & (seg == 0))
    def _():
        for chunk in range(chunks):

            @pl.when(chunk_band(chunk) != band)
            def _():
                greet(0, chunk_band(chunk))

    @pl.when(works)
    def _():
        greet(seg + 1, band)

    @pl.when(works & (seg > 0))
    def _():
        greet(seg - 2, band)
        greet(seg - 2, other)

    @pl.when(works & (seg > halfway))
    def _():
        greet(tail - seg, band)
        greet(tail - seg, other)

    @pl.when(works & (seg >= halfway))
    def _():
        greet(last - seg, band)

    for m in range(batches):

        @pl.when((seg != tail) | (band != HALVES * m + own_half))
        def _():
            greet(tail, HALVES * m + own_half)

    def one_if(condition):
        return jnp.where(condition, 1, 0).astype(jnp.int32)

    def pix_chunk(worker):
        return band if worker % HALVES == 0 else bands - 1 - band

    def pix_sends(worker):
        return (seg == 0) & (pix_chunk(worker) < chunks) & (band != worker)

    expected = one_if(works & (seg < tail)) * 2 + one_if(works & (seg < halfway - 2)) * 2
    expected += one_if(feeds) + one_if(feeds & (seg < halfway))
    for worker in range(workers):
        expected += one_if(pix_sends(worker))
    expected += one_if(works & (seg == tail)) * (
        segments * half_bands - one_if(own_half == lower)
    )

    @pl.when(expected > 0)
    def _():
        pl.semaphore_wait(barrier, expected)

    def pix_copy(worker):
        return pltpu.make_async_remote_copy(
            src_ref=pix_ref.at[worker // HALVES],
            dst_ref=pix_buf.at[pix_chunk(worker)],
            send_sem=pix_send.at[worker],
            recv_sem=pix_recv.at[pix_chunk(worker)],
            device_id=(0, worker),
            device_id_type=MESH,
        )

    own_chunk = band + lower * (bands - 1 - 2 * band)
    for worker in range(workers):

        @pl.when(pix_sends(worker))
        def _():
            pix_copy(worker).start()

    @pl.when(works & (seg == 0) & (own_chunk < chunks))
    def _():
        pltpu.make_async_copy(
            pix_ref.at[micro], pix_buf.at[own_chunk], pix_recv.at[own_chunk]
        ).start()

    def feed_copy(layer, dy):
        return pltpu.make_async_remote_copy(
            src_ref=conv_ref.at[layer, dy],
            dst_ref=weight_buf.at[layers + layer, dy + lower * (2 - 2 * dy)],
            send_sem=feed_send.at[layer, dy],
            recv_sem=feed_recv.at[layer, dy],
            device_id=(seg - 1, band),
            device_id_type=MESH,
        )

    def join_send(slot, to_seg, buffer, at):
        return pltpu.make_async_remote_copy(
            src_ref=join_ref,
            dst_ref=buffer.at[at],
            send_sem=mirror_send.at[slot],
            recv_sem=mirror_recv.at[slot],
            device_id=(to_seg, band),
            device_id_type=MESH,
        )

    second_own = join_send(0, seg - 1, own_join, 1)
    first_mirror = join_send(1, last - seg, mirror_join, 0)
    second_mirror = join_send(2, tail - seg, mirror_join, 1)

    @pl.when(feeds)
    def _():
        for layer in range(layers):
            for dy in range(3):
                feed_copy(layer, dy).start()

    @pl.when(feeds & (seg >= halfway))
    def _():
        second_own.start()

    @pl.when(feeds & (seg < halfway))
    def _():
        first_mirror.start()

    @pl.when(works & (seg < halfway))
    def _():
        second_mirror.start()

    early_copy = pltpu.make_async_remote_copy(
        src_ref=early_out,
        dst_ref=early_skip,
        send_sem=early_send,
        recv_sem=early_recv,
        device_id=(tail - seg, band),
        device_id_type=MESH,
    )

    def hop_copies(buffer, to_seg, send, recv):
        return (
            pltpu.make_async_remote_copy(
                src_ref=own_out,
                dst_ref=buffer.at[pl.ds(0, own_px)],
                send_sem=send.at[0],
                recv_sem=recv.at[0],
                device_id=(to_seg, band),
                device_id_type=MESH,
            ),
            pltpu.make_async_remote_copy(
                src_ref=halo_out,
                dst_ref=buffer.at[pl.ds(own_px, halo_px)],
                send_sem=send.at[1],
                recv_sem=recv.at[1],
                device_id=(to_seg, other),
                device_id_type=MESH,
            ),
        )

    next_copies = hop_copies(in_buf, seg + 2, in_send, in_recv)
    skip_copies = hop_copies(skip_buf, tail - seg, skip_send, skip_recv)

    def fin_copy(g, k):
        return pltpu.make_async_remote_copy(
            src_ref=fin_src.at[g * half_bands + k],
            dst_ref=fin_dst.at[micro],
            send_sem=fin_send.at[g * half_bands + k],
            recv_sem=fin_recv.at[micro],
            device_id=(g, chunk_band(k)),
            device_id_type=MESH,
        )

    def dot(a, b):
        return jnp.dot(a, b, preferred_element_type=jnp.float32)

    @pl.when(works)
    def _():
        @pl.when(seg == tail)
        def _():
            block_rows = fin_src.shape[1]
            at = lax.broadcasted_iota(jnp.int32, (block_rows, own_px), 0)
            pixel = lax.broadcasted_iota(jnp.int32, (block_rows, own_px), 1)
            row = jnp.zeros_like(at)
            for step in range(1, band_rows):
                row += jnp.where(at >= step * share, 1, 0)
            column = at - row * share
            row = row + lower * (band_rows - 1 - 2 * row)
            inside = at < band_rows * share
            base = row * columns + column
            for g in range(segments):
                for k in range(half_bands):
                    wanted = base + (k * band_rows * columns + g * share)
                    place[g * half_bands + k] = jnp.where(
                        inside & (pixel == wanted), 1.0, 0.0
                    ).astype(jnp.bfloat16)

        hid[...] = jnp.zeros_like(hid)
        wide[pl.ds(0, columns)] = jnp.zeros((columns, 3 * channels), jnp.bfloat16)
        join_copy.wait()

        @pl.when(seg > 0)
        def _():
            for copy in weight_copies:
                copy.wait()

        @pl.when(seg >= halfway)
        def _():
            first_mirror.wait_recv()
            second_mirror.wait_recv()
            second_own.wait_recv()

        @pl.when(seg > halfway)
        def _():
            for copy in skip_copies:
                copy.wait_recv()
            skip_part[...] = dot(skip_buf[...], mirror_join[0])

        def take_input():
            @pl.when(seg == 0)
            def _():
                for chunk in range(chunks):
                    pltpu.make_async_copy(
                        pix_ref.at[0], pix_buf.at[chunk], pix_recv.at[chunk]
                    ).wait()
                for row in range(all_px // columns):
                    within = row % band_rows
                    within = within + lower * (band_rows - 1 - 2 * within)
                    hid[pl.ds(row * columns, columns)] = pix_buf[row // band_rows, within]

            @pl.when(seg > 0)
            def _():
                for copy in next_copies:
                    copy.wait_recv()

            @pl.when((seg > 0) & (seg < halfway))
            def _():
                hid[...] = in_buf[...]

            @pl.when(seg == halfway)
            def _():
                skip_part[...] = dot(in_buf[...], mirror_join[0])

            @pl.when(seg >= halfway)
            def _():
                hid[...] = (skip_part[...] + dot(in_buf[...], own_join[0])).astype(jnp.bfloat16)

        def convolve(layer, count):
            keep = count - columns
            at = lax.broadcasted_iota(
                jnp.int32, (count // columns, columns, channels), 1
            ).reshape(count, channels)
            scaled = unit(hid[pl.ds(0, count)].astype(jnp.float32))
            left = jnp.where(at == 0, 0.0, pltpu.roll(scaled, 1, 0))
            right = jnp.where(at == columns - 1, 0.0, pltpu.roll(scaled, count - 1, 0))
            for dx, part in enumerate((left, scaled, right)):
                wide[pl.ds(columns, count), pl.ds(dx * channels, channels)] = part.astype(
                    jnp.bfloat16
                )
            total = dot(wide[pl.ds(0, keep)], weight_buf[layer, 0])
            for dy in range(1, 3):
                total += dot(wide[pl.ds(dy * columns, keep)], weight_buf[layer, dy])
            hid[pl.ds(0, keep)] = (
                hid[pl.ds(0, keep)].astype(jnp.float32) + jnp.maximum(total, 0.0)
            ).astype(jnp.bfloat16)

        def first_section(index, carry):
            @pl.when(index == 1)
            def _():
                take_input()

            layer = jnp.maximum(index - 1, 0)

            @pl.when(seg == 0)
            def _():
                for dy in range(3):
                    pltpu.make_async_copy(
                        conv_ref.at[layer, dy], weight_buf.at[layer, dy], weight_sem.at[layer, dy]
                    ).wait()

            convolve(layer, all_px)
            return carry

        lax.fori_loop(one_if(seg == 0), layers + 1, first_section, 0)
        mid_px = early_out.shape[0]

        @pl.when(seg < halfway)
        def _():
            early_out[...] = hid[pl.ds(0, mid_px)]
            early_copy.start()

        @pl.when(seg >= halfway)
        def _():
            early_copy.wait_recv()
            hid[pl.ds(0, mid_px)] = (
                dot(early_skip[...], mirror_join[1]) + dot(hid[pl.ds(0, mid_px)], own_join[1])
            ).astype(jnp.bfloat16)

        def second_section(layer, carry):
            for dy in range(3):
                feed_copy(layer, dy).wait_recv()
            convolve(layers + layer, mid_px)
            return carry

        lax.fori_loop(0, layers, second_section, 0)
        hidden = hid[pl.ds(0, own_px)]

        @pl.when(seg < tail)
        def _():
            for row in range(halo_px // columns):
                start = own_px - (row + 1) * columns
                halo_out[pl.ds(row * columns, columns)] = hidden[start : start + columns]
            own_out[...] = hidden
            for copy in next_copies[::-1]:
                copy.start()

            @pl.when(seg < halfway - 2)
            def _():
                for copy in skip_copies:
                    copy.start()

        @pl.when(seg == tail)
        def _():
            decoded = unit(hidden.astype(jnp.float32)).astype(jnp.bfloat16)
            sorting = place[...].reshape(-1, own_px)
            fin_src[...] = dot(sorting, decoded).astype(jnp.bfloat16).reshape(fin_src.shape)
            for g in range(segments):
                for k in range(half_bands):
                    if g != tail:
                        fin_copy(g, k).start()
                    else:
                        here = chunk_band(k) == band

                        @pl.when(here)
                        def _():
                            pltpu.make_async_copy(
                                fin_src.at[g * half_bands + k],
                                fin_dst.at[micro],
                                fin_recv.at[micro],
                            ).start()

                        @pl.when(jnp.logical_not(here))
                        def _():
                            fin_copy(g, k).start()

    for m in range(batches):
        pltpu.make_async_copy(fin_src.at[0], fin_dst.at[m], fin_recv.at[m]).wait()
    out_ref[...] = fin_dst[:, : out_ref.shape[1]]

    for worker in range(workers):

        @pl.when(pix_sends(worker))
        def _():
            pix_copy(worker).wait_send()

    @pl.when(works & (seg < halfway))
    def _():
        second_mirror.wait_send()
        early_copy.wait_send()

    @pl.when(feeds)
    def _():
        for layer in range(layers):
            for dy in range(3):
                feed_copy(layer, dy).wait_send()

    @pl.when(feeds & (seg >= halfway))
    def _():
        second_own.wait_send()

    @pl.when(feeds & (seg < halfway))
    def _():
        first_mirror.wait_send()

    @pl.when(works & (seg < tail))
    def _():
        for copy in next_copies:
            copy.wait_send()

    @pl.when(works & (seg < halfway - 2))
    def _():
        for copy in skip_copies:
            copy.wait_send()

    @pl.when(works & (seg == tail))
    def _():
        for g in range(segments):
            for k in range(half_bands):
                if g != tail:
                    fin_copy(g, k).wait_send()
                else:

                    @pl.when(chunk_band(k) != band)
                    def _():
                        fin_copy(g, k).wait_send()


def shards(segments, bands, pixels, conv_weight, join_weight):
    batches, band_rows, columns, channels = pixels.shape
    layers = conv_weight.shape[1]
    own_rows = band_rows * bands // HALVES
    rows = own_rows + 2 * layers
    chunks = -(-rows // band_rows)
    own_px, halo_px, all_px = own_rows * columns, 2 * layers * columns, rows * columns
    mid_px = (own_rows + layers) * columns
    share = columns // segments
    piece = band_rows * share
    block_rows = -(-piece // 16) * 16
    blocks = segments * (bands // HALVES)
    workers = HALVES * batches
    kept = jnp.bfloat16
    conv = conv_weight.reshape(layers, 3, 3 * channels, channels)
    join = join_weight.reshape(channels, channels)
    dma = pltpu.SemaphoreType.DMA
    result = pl.pallas_call(
        functools.partial(kernel, segments, bands),
        out_shape=jax.ShapeDtypeStruct((batches, piece, channels), kept),
        in_specs=[pl.BlockSpec(memory_space=pltpu.HBM)] * 3,
        out_specs=pl.BlockSpec(memory_space=pltpu.VMEM),
        scratch_shapes=[
            pltpu.VMEM((chunks, band_rows, columns, channels), kept),
            pltpu.VMEM((all_px, channels), kept),
            pltpu.VMEM((all_px, channels), kept),
            pltpu.VMEM((mid_px, channels), kept),
            pltpu.VMEM((mid_px, channels), kept),
            pltpu.VMEM((2 * layers, 3, 3 * channels, channels), kept),
            pltpu.VMEM((2, channels, channels), kept),
            pltpu.VMEM((2, channels, channels), kept),
            pltpu.VMEM((all_px, channels), jnp.float32),
            pltpu.VMEM((all_px, channels), kept),
            pltpu.VMEM((all_px + columns, 3 * channels), kept),
            pltpu.VMEM((own_px, channels), kept),
            pltpu.VMEM((halo_px, channels), kept),
            pltpu.VMEM((blocks, block_rows, own_px), kept),
            pltpu.VMEM((blocks, block_rows, channels), kept),
            pltpu.VMEM((batches, block_rows, channels), kept),
            dma((layers, 3)),
            dma,
            dma((workers,)),
            dma((chunks,)),
            dma((2,)),
            dma((2,)),
            dma((2,)),
            dma((2,)),
            dma((3,)),
            dma((3,)),
            dma((layers, 3)),
            dma((layers, 3)),
            dma,
            dma,
            dma((blocks,)),
            dma((batches,)),
        ],
        compiler_params=pltpu.CompilerParams(collective_id=0, has_side_effects=True),
    )(pixels, conv, join)
    return result.reshape(batches, band_rows, share, channels)


def solution(mesh):
    return jax.shard_map(
        functools.partial(shards, mesh.shape["segment"], mesh.shape["band"]),
        mesh=mesh,
        in_specs=(
            P(None, "band", None, None),
            P("segment", None, None, None, None, None),
            P("segment", None, None),
        ),
        out_specs=P(None, "band", "segment", None),
        check_vma=False,
    )
```

```python
import functools

import jax
import jax.numpy as jnp
from jax import lax
from jax.experimental import pallas as pl
from jax.experimental.pallas import tpu as pltpu
from jax.sharding import PartitionSpec as P

MESH = pl.DeviceIdType.MESH
HALVES = 2


def unit(values):
    return values * lax.rsqrt(jnp.mean(values * values, axis=-1, keepdims=True) + 1e-05)


def kernel(
    segments,
    bands,
    pix_ref,
    conv_ref,
    join_ref,
    out_ref,
    pix_buf,
    in_buf,
    skip_buf,
    early_skip,
    early_out,
    weight_buf,
    own_join,
    mirror_join,
    skip_part,
    hid,
    wide,
    own_out,
    halo_out,
    place,
    fin_src,
    fin_dst,
    weight_sem,
    join_sem,
    pix_send,
    pix_recv,
    in_send,
    in_recv,
    skip_send,
    skip_recv,
    mirror_send,
    mirror_recv,
    feed_send,
    feed_recv,
    early_send,
    early_recv,
    fin_send,
    fin_recv,
):
    batches, band_rows, columns, channels = pix_ref.shape
    layers = conv_ref.shape[0]
    workers = HALVES * batches
    chunks = pix_buf.shape[0]
    own_px = own_out.shape[0]
    halo_px = halo_out.shape[0]
    all_px = own_px + halo_px
    half_bands = bands // HALVES
    halfway = segments // 2
    last = segments - 1
    tail = segments - 2
    share = columns // segments
    seg = lax.axis_index("segment")
    band = lax.axis_index("band")
    lower = lax.rem(band, HALVES)
    micro = lax.div(band, HALVES)
    other = band + 1 - 2 * lower
    works = (band < workers) & (lax.rem(seg, 2) == 0)
    feeds = (band < workers) & (lax.rem(seg, 2) == 1)
    own_half = lax.div(band, half_bands)

    weight_copies = []
    for layer in range(layers):
        for dy in range(3):
            to = dy + lower * (2 - 2 * dy)
            weight_copies.append(
                pltpu.make_async_copy(
                    conv_ref.at[layer, dy], weight_buf.at[layer, to], weight_sem.at[layer, dy]
                )
            )
    join_copy = pltpu.make_async_copy(join_ref, own_join.at[0], join_sem)

    @pl.when(works)
    def _():
        for copy in weight_copies:
            copy.start()
        join_copy.start()

    barrier = pltpu.get_barrier_semaphore()

    def greet(to_seg, to_band):
        pl.semaphore_signal(barrier, inc=1, device_id=(to_seg, to_band), device_id_type=MESH)

    def chunk_band(chunk):
        return chunk + lower * (bands - 1 - 2 * chunk)

    @pl.when(works & (seg == 0))
    def _():
        for chunk in range(chunks):

            @pl.when(chunk_band(chunk) != band)
            def _():
                greet(0, chunk_band(chunk))

    @pl.when(works)
    def _():
        greet(seg + 1, band)

    @pl.when(works & (seg > 0))
    def _():
        greet(seg - 2, band)
        greet(seg - 2, other)

    @pl.when(works & (seg > halfway))
    def _():
        greet(tail - seg, band)
        greet(tail - seg, other)

    @pl.when(works & (seg >= halfway))
    def _():
        greet(last - seg, band)

    for m in range(batches):

        @pl.when((seg != tail) | (band != HALVES * m + own_half))
        def _():
            greet(tail, HALVES * m + own_half)

    def one_if(condition):
        return jnp.where(condition, 1, 0).astype(jnp.int32)

    def pix_chunk(worker):
        return band if worker % HALVES == 0 else bands - 1 - band

    def pix_sends(worker):
        return (seg == 0) & (pix_chunk(worker) < chunks) & (band != worker)

    expected = one_if(works & (seg < tail)) * 2 + one_if(works & (seg < halfway - 2)) * 2
    expected += one_if(feeds) + one_if(feeds & (seg < halfway))
    for worker in range(workers):
        expected += one_if(pix_sends(worker))
    expected += one_if(works & (seg == tail)) * (
        segments * half_bands - one_if(own_half == lower)
    )

    @pl.when(expected > 0)
    def _():
        pl.semaphore_wait(barrier, expected)

    def pix_copy(worker):
        return pltpu.make_async_remote_copy(
            src_ref=pix_ref.at[worker // HALVES],
            dst_ref=pix_buf.at[pix_chunk(worker)],
            send_sem=pix_send.at[worker],
            recv_sem=pix_recv.at[pix_chunk(worker)],
            device_id=(0, worker),
            device_id_type=MESH,
        )

    own_chunk = band + lower * (bands - 1 - 2 * band)
    for worker in range(workers):

        @pl.when(pix_sends(worker))
        def _():
            pix_copy(worker).start()

    @pl.when(works & (seg == 0) & (own_chunk < chunks))
    def _():
        pltpu.make_async_copy(
            pix_ref.at[micro], pix_buf.at[own_chunk], pix_recv.at[own_chunk]
        ).start()

    def feed_copy(layer, dy):
        return pltpu.make_async_remote_copy(
            src_ref=conv_ref.at[layer, dy],
            dst_ref=weight_buf.at[layers + layer, dy + lower * (2 - 2 * dy)],
            send_sem=feed_send.at[layer, dy],
            recv_sem=feed_recv.at[layer, dy],
            device_id=(seg - 1, band),
            device_id_type=MESH,
        )

    def join_send(slot, to_seg, buffer, at):
        return pltpu.make_async_remote_copy(
            src_ref=join_ref,
            dst_ref=buffer.at[at],
            send_sem=mirror_send.at[slot],
            recv_sem=mirror_recv.at[slot],
            device_id=(to_seg, band),
            device_id_type=MESH,
        )

    second_own = join_send(0, seg - 1, own_join, 1)
    first_mirror = join_send(1, last - seg, mirror_join, 0)
    second_mirror = join_send(2, tail - seg, mirror_join, 1)

    @pl.when(feeds)
    def _():
        for layer in range(layers):
            for dy in range(3):
                feed_copy(layer, dy).start()

    @pl.when(feeds & (seg >= halfway))
    def _():
        second_own.start()

    @pl.when(feeds & (seg < halfway))
    def _():
        first_mirror.start()

    @pl.when(works & (seg < halfway))
    def _():
        second_mirror.start()

    early_copy = pltpu.make_async_remote_copy(
        src_ref=early_out,
        dst_ref=early_skip,
        send_sem=early_send,
        recv_sem=early_recv,
        device_id=(tail - seg, band),
        device_id_type=MESH,
    )

    def hop_copies(buffer, to_seg, send, recv):
        return (
            pltpu.make_async_remote_copy(
                src_ref=own_out,
                dst_ref=buffer.at[pl.ds(0, own_px)],
                send_sem=send.at[0],
                recv_sem=recv.at[0],
                device_id=(to_seg, band),
                device_id_type=MESH,
            ),
            pltpu.make_async_remote_copy(
                src_ref=halo_out,
                dst_ref=buffer.at[pl.ds(own_px, halo_px)],
                send_sem=send.at[1],
                recv_sem=recv.at[1],
                device_id=(to_seg, other),
                device_id_type=MESH,
            ),
        )

    next_copies = hop_copies(in_buf, seg + 2, in_send, in_recv)
    skip_copies = hop_copies(skip_buf, tail - seg, skip_send, skip_recv)

    def fin_copy(g, k):
        return pltpu.make_async_remote_copy(
            src_ref=fin_src.at[g * half_bands + k],
            dst_ref=fin_dst.at[micro],
            send_sem=fin_send.at[g * half_bands + k],
            recv_sem=fin_recv.at[micro],
            device_id=(g, chunk_band(k)),
            device_id_type=MESH,
        )

    def dot(a, b):
        return jnp.dot(a, b, preferred_element_type=jnp.float32)

    @pl.when(works)
    def _():
        @pl.when(seg == tail)
        def _():
            block_rows = fin_src.shape[1]
            at = lax.broadcasted_iota(jnp.int32, (block_rows, own_px), 0)
            pixel = lax.broadcasted_iota(jnp.int32, (block_rows, own_px), 1)
            row = jnp.zeros_like(at)
            for step in range(1, band_rows):
                row += jnp.where(at >= step * share, 1, 0)
            column = at - row * share
            row = row + lower * (band_rows - 1 - 2 * row)
            inside = at < band_rows * share
            base = row * columns + column
            for g in range(segments):
                for k in range(half_bands):
                    wanted = base + (k * band_rows * columns + g * share)
                    place[g * half_bands + k] = jnp.where(
                        inside & (pixel == wanted), 1.0, 0.0
                    ).astype(jnp.bfloat16)

        hid[...] = jnp.zeros_like(hid)
        wide[pl.ds(0, columns)] = jnp.zeros((columns, 3 * channels), jnp.bfloat16)
        join_copy.wait()

        @pl.when(seg > 0)
        def _():
            for copy in weight_copies:
                copy.wait()

        @pl.when(seg >= halfway)
        def _():
            first_mirror.wait_recv()
            second_mirror.wait_recv()
            second_own.wait_recv()

        @pl.when(seg > halfway)
        def _():
            for copy in skip_copies:
                copy.wait_recv()
            skip_part[...] = dot(skip_buf[...], mirror_join[0])

        def take_input():
            @pl.when(seg == 0)
            def _():
                for chunk in range(chunks):
                    pltpu.make_async_copy(
                        pix_ref.at[0], pix_buf.at[chunk], pix_recv.at[chunk]
                    ).wait()
                for row in range(all_px // columns):
                    within = row % band_rows
                    within = within + lower * (band_rows - 1 - 2 * within)
                    hid[pl.ds(row * columns, columns)] = pix_buf[row // band_rows, within]

            @pl.when(seg > 0)
            def _():
                for copy in next_copies:
                    copy.wait_recv()

            @pl.when((seg > 0) & (seg < halfway))
            def _():
                hid[...] = in_buf[...]

            @pl.when(seg == halfway)
            def _():
                skip_part[...] = dot(in_buf[...], mirror_join[0])

            @pl.when(seg >= halfway)
            def _():
                hid[...] = (skip_part[...] + dot(in_buf[...], own_join[0])).astype(jnp.bfloat16)

        def convolve(layer, count):
            keep = count - columns
            at = lax.broadcasted_iota(
                jnp.int32, (count // columns, columns, channels), 1
            ).reshape(count, channels)
            scaled = unit(hid[pl.ds(0, count)].astype(jnp.float32))
            left = jnp.where(at == 0, 0.0, pltpu.roll(scaled, 1, 0))
            right = jnp.where(at == columns - 1, 0.0, pltpu.roll(scaled, count - 1, 0))
            for dx, part in enumerate((left, scaled, right)):
                wide[pl.ds(columns, count), pl.ds(dx * channels, channels)] = part.astype(
                    jnp.bfloat16
                )
            total = dot(wide[pl.ds(0, keep)], weight_buf[layer, 0])
            for dy in range(1, 3):
                total += dot(wide[pl.ds(dy * columns, keep)], weight_buf[layer, dy])
            hid[pl.ds(0, keep)] = (
                hid[pl.ds(0, keep)].astype(jnp.float32) + jnp.maximum(total, 0.0)
            ).astype(jnp.bfloat16)

        mid_px = early_out.shape[0]

        def both_sections(turn, carry):
            real = turn == 1
            count = jnp.where(real, layers, 1)

            @pl.when(real)
            def _():
                take_input()

            def first_section(layer, inner):
                @pl.when(seg == 0)
                def _():
                    for dy in range(3):
                        pltpu.make_async_copy(
                            conv_ref.at[layer, dy],
                            weight_buf.at[layer, dy],
                            weight_sem.at[layer, dy],
                        ).wait()

                convolve(layer, all_px)
                return inner

            lax.fori_loop(0, count, first_section, 0)

            @pl.when(real & (seg < halfway))
            def _():
                early_out[...] = hid[pl.ds(0, mid_px)]
                early_copy.start()

            @pl.when(real & (seg >= halfway))
            def _():
                early_copy.wait_recv()
                hid[pl.ds(0, mid_px)] = (
                    dot(early_skip[...], mirror_join[1]) + dot(hid[pl.ds(0, mid_px)], own_join[1])
                ).astype(jnp.bfloat16)

            def second_section(layer, inner):
                @pl.when(real)
                def _():
                    for dy in range(3):
                        feed_copy(layer, dy).wait_recv()

                convolve(layer + jnp.where(real, layers, 0), mid_px)
                return inner

            lax.fori_loop(0, count, second_section, 0)
            return carry

        lax.fori_loop(one_if(seg == 0), 2, both_sections, 0)
        hidden = hid[pl.ds(0, own_px)]

        @pl.when(seg < tail)
        def _():
            for row in range(halo_px // columns):
                start = own_px - (row + 1) * columns
                halo_out[pl.ds(row * columns, columns)] = hidden[start : start + columns]
            own_out[...] = hidden
            for copy in next_copies[::-1]:
                copy.start()

            @pl.when(seg < halfway - 2)
            def _():
                for copy in skip_copies:
                    copy.start()

        @pl.when(seg == tail)
        def _():
            decoded = unit(hidden.astype(jnp.float32)).astype(jnp.bfloat16)
            sorting = place[...].reshape(-1, own_px)
            fin_src[...] = dot(sorting, decoded).astype(jnp.bfloat16).reshape(fin_src.shape)
            for g in range(segments):
                for k in range(half_bands):
                    if g != tail:
                        fin_copy(g, k).start()
                    else:
                        here = chunk_band(k) == band

                        @pl.when(here)
                        def _():
                            pltpu.make_async_copy(
                                fin_src.at[g * half_bands + k],
                                fin_dst.at[micro],
                                fin_recv.at[micro],
                            ).start()

                        @pl.when(jnp.logical_not(here))
                        def _():
                            fin_copy(g, k).start()

    for m in range(batches):
        pltpu.make_async_copy(fin_src.at[0], fin_dst.at[m], fin_recv.at[m]).wait()
    out_ref[...] = fin_dst[:, : out_ref.shape[1]]

    for worker in range(workers):

        @pl.when(pix_sends(worker))
        def _():
            pix_copy(worker).wait_send()

    @pl.when(works & (seg < halfway))
    def _():
        second_mirror.wait_send()
        early_copy.wait_send()

    @pl.when(feeds)
    def _():
        for layer in range(layers):
            for dy in range(3):
                feed_copy(layer, dy).wait_send()

    @pl.when(feeds & (seg >= halfway))
    def _():
        second_own.wait_send()

    @pl.when(feeds & (seg < halfway))
    def _():
        first_mirror.wait_send()

    @pl.when(works & (seg < tail))
    def _():
        for copy in next_copies:
            copy.wait_send()

    @pl.when(works & (seg < halfway - 2))
    def _():
        for copy in skip_copies:
            copy.wait_send()

    @pl.when(works & (seg == tail))
    def _():
        for g in range(segments):
            for k in range(half_bands):
                if g != tail:
                    fin_copy(g, k).wait_send()
                else:

                    @pl.when(chunk_band(k) != band)
                    def _():
                        fin_copy(g, k).wait_send()


def shards(segments, bands, pixels, conv_weight, join_weight):
    batches, band_rows, columns, channels = pixels.shape
    layers = conv_weight.shape[1]
    own_rows = band_rows * bands // HALVES
    rows = own_rows + 2 * layers
    chunks = -(-rows // band_rows)
    own_px, halo_px, all_px = own_rows * columns, 2 * layers * columns, rows * columns
    mid_px = (own_rows + layers) * columns
    share = columns // segments
    piece = band_rows * share
    block_rows = -(-piece // 16) * 16
    blocks = segments * (bands // HALVES)
    workers = HALVES * batches
    kept = jnp.bfloat16
    conv = conv_weight.reshape(layers, 3, 3 * channels, channels)
    join = join_weight.reshape(channels, channels)
    dma = pltpu.SemaphoreType.DMA
    result = pl.pallas_call(
        functools.partial(kernel, segments, bands),
        out_shape=jax.ShapeDtypeStruct((batches, piece, channels), kept),
        in_specs=[pl.BlockSpec(memory_space=pltpu.HBM)] * 3,
        out_specs=pl.BlockSpec(memory_space=pltpu.VMEM),
        scratch_shapes=[
            pltpu.VMEM((chunks, band_rows, columns, channels), kept),
            pltpu.VMEM((all_px, channels), kept),
            pltpu.VMEM((all_px, channels), kept),
            pltpu.VMEM((mid_px, channels), kept),
            pltpu.VMEM((mid_px, channels), kept),
            pltpu.VMEM((2 * layers, 3, 3 * channels, channels), kept),
            pltpu.VMEM((2, channels, channels), kept),
            pltpu.VMEM((2, channels, channels), kept),
            pltpu.VMEM((all_px, channels), jnp.float32),
            pltpu.VMEM((all_px, channels), kept),
            pltpu.VMEM((all_px + columns, 3 * channels), kept),
            pltpu.VMEM((own_px, channels), kept),
            pltpu.VMEM((halo_px, channels), kept),
            pltpu.VMEM((blocks, block_rows, own_px), kept),
            pltpu.VMEM((blocks, block_rows, channels), kept),
            pltpu.VMEM((batches, block_rows, channels), kept),
            dma((layers, 3)),
            dma,
            dma((workers,)),
            dma((chunks,)),
            dma((2,)),
            dma((2,)),
            dma((2,)),
            dma((2,)),
            dma((3,)),
            dma((3,)),
            dma((layers, 3)),
            dma((layers, 3)),
            dma,
            dma,
            dma((blocks,)),
            dma((batches,)),
        ],
        compiler_params=pltpu.CompilerParams(collective_id=0, has_side_effects=True),
    )(pixels, conv, join)
    return result.reshape(batches, band_rows, share, channels)


def solution(mesh):
    return jax.shard_map(
        functools.partial(shards, mesh.shape["segment"], mesh.shape["band"]),
        mesh=mesh,
        in_specs=(
            P(None, "band", None, None),
            P("segment", None, None, None, None, None),
            P("segment", None, None),
        ),
        out_specs=P(None, "band", "segment", None),
        check_vma=False,
    )
```

```python
import functools

import jax
import jax.numpy as jnp
from jax import lax
from jax.experimental import pallas as pl
from jax.experimental.pallas import tpu as pltpu
from jax.sharding import PartitionSpec as P

MESH = pl.DeviceIdType.MESH
HALVES = 2


def unit(values):
    return values * lax.rsqrt(jnp.mean(values * values, axis=-1, keepdims=True) + 1e-05)


def kernel(
    segments,
    bands,
    pix_ref,
    conv_ref,
    join_ref,
    out_ref,
    pix_buf,
    in_buf,
    skip_buf,
    early_skip,
    early_out,
    weight_buf,
    own_join,
    mirror_join,
    skip_part,
    hid,
    wide,
    own_out,
    halo_out,
    place,
    fin_src,
    fin_dst,
    weight_sem,
    join_sem,
    pix_send,
    pix_recv,
    in_send,
    in_recv,
    skip_send,
    skip_recv,
    mirror_send,
    mirror_recv,
    feed_send,
    feed_recv,
    early_send,
    early_recv,
    fin_send,
    fin_recv,
):
    batches, band_rows, columns, channels = pix_ref.shape
    layers = conv_ref.shape[0]
    workers = HALVES * batches
    chunks = pix_buf.shape[0]
    own_px = own_out.shape[0]
    halo_px = halo_out.shape[0]
    all_px = own_px + halo_px
    half_bands = bands // HALVES
    halfway = segments // 2
    last = segments - 1
    tail = segments - 2
    share = columns // segments
    seg = lax.axis_index("segment")
    band = lax.axis_index("band")
    lower = lax.rem(band, HALVES)
    micro = lax.div(band, HALVES)
    other = band + 1 - 2 * lower
    works = (band < workers) & (lax.rem(seg, 2) == 0)
    feeds = (band < workers) & (lax.rem(seg, 2) == 1)
    own_half = lax.div(band, half_bands)

    weight_copies = []
    for layer in range(layers):
        for dy in range(3):
            to = dy + lower * (2 - 2 * dy)
            weight_copies.append(
                pltpu.make_async_copy(
                    conv_ref.at[layer, dy], weight_buf.at[layer, to], weight_sem.at[layer, dy]
                )
            )
    join_copy = pltpu.make_async_copy(join_ref, own_join.at[0], join_sem)

    @pl.when(works)
    def _():
        for copy in weight_copies:
            copy.start()
        join_copy.start()

    barrier = pltpu.get_barrier_semaphore()

    def greet(to_seg, to_band):
        pl.semaphore_signal(barrier, inc=1, device_id=(to_seg, to_band), device_id_type=MESH)

    def chunk_band(chunk):
        return chunk + lower * (bands - 1 - 2 * chunk)

    @pl.when(works & (seg == 0))
    def _():
        for chunk in range(chunks):

            @pl.when(chunk_band(chunk) != band)
            def _():
                greet(0, chunk_band(chunk))

    @pl.when(works)
    def _():
        greet(seg + 1, band)

    @pl.when(works & (seg > 0))
    def _():
        greet(seg - 2, band)
        greet(seg - 2, other)

    @pl.when(works & (seg > halfway))
    def _():
        greet(tail - seg, band)
        greet(tail - seg, other)

    @pl.when(works & (seg >= halfway))
    def _():
        greet(last - seg, band)

    for m in range(batches):

        @pl.when((seg != tail) | (band != HALVES * m + own_half))
        def _():
            greet(tail, HALVES * m + own_half)

    def one_if(condition):
        return jnp.where(condition, 1, 0).astype(jnp.int32)

    def pix_chunk(worker):
        return band if worker % HALVES == 0 else bands - 1 - band

    def pix_sends(worker):
        return (seg == 0) & (pix_chunk(worker) < chunks) & (band != worker)

    expected = one_if(works & (seg < tail)) * 2 + one_if(works & (seg < halfway - 2)) * 2
    expected += one_if(feeds) + one_if(feeds & (seg < halfway))
    for worker in range(workers):
        expected += one_if(pix_sends(worker))
    expected += one_if(works & (seg == tail)) * (
        segments * half_bands - one_if(own_half == lower)
    )

    @pl.when(expected > 0)
    def _():
        pl.semaphore_wait(barrier, expected)

    def pix_copy(worker):
        return pltpu.make_async_remote_copy(
            src_ref=pix_ref.at[worker // HALVES],
            dst_ref=pix_buf.at[pix_chunk(worker)],
            send_sem=pix_send.at[worker],
            recv_sem=pix_recv.at[pix_chunk(worker)],
            device_id=(0, worker),
            device_id_type=MESH,
        )

    own_chunk = band + lower * (bands - 1 - 2 * band)
    for worker in range(workers):

        @pl.when(pix_sends(worker))
        def _():
            pix_copy(worker).start()

    @pl.when(works & (seg == 0) & (own_chunk < chunks))
    def _():
        pltpu.make_async_copy(
            pix_ref.at[micro], pix_buf.at[own_chunk], pix_recv.at[own_chunk]
        ).start()

    def feed_copy(layer, dy):
        return pltpu.make_async_remote_copy(
            src_ref=conv_ref.at[layer, dy],
            dst_ref=weight_buf.at[layers + layer, dy + lower * (2 - 2 * dy)],
            send_sem=feed_send.at[layer, dy],
            recv_sem=feed_recv.at[layer, dy],
            device_id=(seg - 1, band),
            device_id_type=MESH,
        )

    def join_send(slot, to_seg, buffer, at):
        return pltpu.make_async_remote_copy(
            src_ref=join_ref,
            dst_ref=buffer.at[at],
            send_sem=mirror_send.at[slot],
            recv_sem=mirror_recv.at[slot],
            device_id=(to_seg, band),
            device_id_type=MESH,
        )

    second_own = join_send(0, seg - 1, own_join, 1)
    first_mirror = join_send(1, last - seg, mirror_join, 0)
    second_mirror = join_send(2, tail - seg, mirror_join, 1)

    @pl.when(feeds)
    def _():
        for layer in range(layers):
            for dy in range(3):
                feed_copy(layer, dy).start()

    @pl.when(feeds & (seg >= halfway))
    def _():
        second_own.start()

    @pl.when(feeds & (seg < halfway))
    def _():
        first_mirror.start()

    @pl.when(works & (seg < halfway))
    def _():
        second_mirror.start()

    early_copy = pltpu.make_async_remote_copy(
        src_ref=early_out,
        dst_ref=early_skip,
        send_sem=early_send,
        recv_sem=early_recv,
        device_id=(tail - seg, band),
        device_id_type=MESH,
    )

    def hop_copies(buffer, to_seg, send, recv):
        return (
            pltpu.make_async_remote_copy(
                src_ref=own_out,
                dst_ref=buffer.at[pl.ds(0, own_px)],
                send_sem=send.at[0],
                recv_sem=recv.at[0],
                device_id=(to_seg, band),
                device_id_type=MESH,
            ),
            pltpu.make_async_remote_copy(
                src_ref=halo_out,
                dst_ref=buffer.at[pl.ds(own_px, halo_px)],
                send_sem=send.at[1],
                recv_sem=recv.at[1],
                device_id=(to_seg, other),
                device_id_type=MESH,
            ),
        )

    next_copies = hop_copies(in_buf, seg + 2, in_send, in_recv)
    skip_copies = hop_copies(skip_buf, tail - seg, skip_send, skip_recv)

    def fin_copy(g, k):
        return pltpu.make_async_remote_copy(
            src_ref=fin_src.at[g * half_bands + k],
            dst_ref=fin_dst.at[micro],
            send_sem=fin_send.at[g * half_bands + k],
            recv_sem=fin_recv.at[micro],
            device_id=(g, chunk_band(k)),
            device_id_type=MESH,
        )

    def dot(a, b):
        return jnp.dot(a, b, preferred_element_type=jnp.float32)

    @pl.when(works)
    def _():
        @pl.when(seg == tail)
        def _():
            block_rows = fin_src.shape[1]
            at = lax.broadcasted_iota(jnp.int32, (block_rows, own_px), 0)
            pixel = lax.broadcasted_iota(jnp.int32, (block_rows, own_px), 1)
            row = jnp.zeros_like(at)
            for step in range(1, band_rows):
                row += jnp.where(at >= step * share, 1, 0)
            column = at - row * share
            row = row + lower * (band_rows - 1 - 2 * row)
            inside = at < band_rows * share
            base = row * columns + column
            for g in range(segments):
                for k in range(half_bands):
                    wanted = base + (k * band_rows * columns + g * share)
                    place[g * half_bands + k] = jnp.where(
                        inside & (pixel == wanted), 1.0, 0.0
                    ).astype(jnp.bfloat16)

        wide[pl.ds(0, columns)] = jnp.zeros((columns, 3 * channels), jnp.bfloat16)
        join_copy.wait()

        for copy in weight_copies:
            copy.wait()

        @pl.when(seg >= halfway)
        def _():
            first_mirror.wait_recv()
            second_mirror.wait_recv()
            second_own.wait_recv()

        @pl.when(seg > halfway)
        def _():
            for copy in skip_copies:
                copy.wait_recv()
            skip_part[...] = dot(skip_buf[...], mirror_join[0])

        def take_input():
            @pl.when(seg == 0)
            def _():
                for chunk in range(chunks):
                    pltpu.make_async_copy(
                        pix_ref.at[0], pix_buf.at[chunk], pix_recv.at[chunk]
                    ).wait()
                for row in range(all_px // columns):
                    within = row % band_rows
                    within = within + lower * (band_rows - 1 - 2 * within)
                    hid[pl.ds(row * columns, columns)] = pix_buf[row // band_rows, within]

            @pl.when(seg > 0)
            def _():
                for copy in next_copies:
                    copy.wait_recv()

            @pl.when((seg > 0) & (seg < halfway))
            def _():
                hid[...] = in_buf[...]

            @pl.when(seg == halfway)
            def _():
                skip_part[...] = dot(in_buf[...], mirror_join[0])

            @pl.when(seg >= halfway)
            def _():
                hid[...] = (skip_part[...] + dot(in_buf[...], own_join[0])).astype(jnp.bfloat16)

        def convolve(layer, count):
            keep = count - columns
            at = lax.broadcasted_iota(
                jnp.int32, (count // columns, columns, channels), 1
            ).reshape(count, channels)
            scaled = unit(hid[pl.ds(0, count)].astype(jnp.float32))
            left = jnp.where(at == 0, 0.0, pltpu.roll(scaled, 1, 0))
            right = jnp.where(at == columns - 1, 0.0, pltpu.roll(scaled, count - 1, 0))
            for dx, part in enumerate((left, scaled, right)):
                wide[pl.ds(columns, count), pl.ds(dx * channels, channels)] = part.astype(
                    jnp.bfloat16
                )
            total = dot(wide[pl.ds(0, keep)], weight_buf[layer, 0])
            for dy in range(1, 3):
                total += dot(wide[pl.ds(dy * columns, keep)], weight_buf[layer, dy])
            hid[pl.ds(0, keep)] = (
                hid[pl.ds(0, keep)].astype(jnp.float32) + jnp.maximum(total, 0.0)
            ).astype(jnp.bfloat16)

        mid_px = early_out.shape[0]

        take_input()
        for layer in range(layers):
            convolve(layer, all_px - layer * columns)

        @pl.when(seg < halfway)
        def _():
            early_out[...] = hid[pl.ds(0, mid_px)]
            early_copy.start()

        @pl.when(seg >= halfway)
        def _():
            early_copy.wait_recv()
            hid[pl.ds(0, mid_px)] = (
                dot(early_skip[...], mirror_join[1]) + dot(hid[pl.ds(0, mid_px)], own_join[1])
            ).astype(jnp.bfloat16)

        for layer in range(layers):
            for dy in range(3):
                feed_copy(layer, dy).wait_recv()
            convolve(layers + layer, mid_px - layer * columns)
        hidden = hid[pl.ds(0, own_px)]

        @pl.when(seg < tail)
        def _():
            for row in range(halo_px // columns):
                start = own_px - (row + 1) * columns
                halo_out[pl.ds(row * columns, columns)] = hidden[start : start + columns]
            own_out[...] = hidden
            for copy in next_copies[::-1]:
                copy.start()

            @pl.when(seg < halfway - 2)
            def _():
                for copy in skip_copies:
                    copy.start()

        @pl.when(seg == tail)
        def _():
            decoded = unit(hidden.astype(jnp.float32)).astype(jnp.bfloat16)
            sorting = place[...].reshape(-1, own_px)
            fin_src[...] = dot(sorting, decoded).astype(jnp.bfloat16).reshape(fin_src.shape)
            for g in range(segments):
                for k in range(half_bands):
                    if g != tail:
                        fin_copy(g, k).start()
                    else:
                        here = chunk_band(k) == band

                        @pl.when(here)
                        def _():
                            pltpu.make_async_copy(
                                fin_src.at[g * half_bands + k],
                                fin_dst.at[micro],
                                fin_recv.at[micro],
                            ).start()

                        @pl.when(jnp.logical_not(here))
                        def _():
                            fin_copy(g, k).start()

    for m in range(batches):
        pltpu.make_async_copy(fin_src.at[0], fin_dst.at[m], fin_recv.at[m]).wait()
    out_ref[...] = fin_dst[:, : out_ref.shape[1]]

    for worker in range(workers):

        @pl.when(pix_sends(worker))
        def _():
            pix_copy(worker).wait_send()

    @pl.when(works & (seg < halfway))
    def _():
        second_mirror.wait_send()
        early_copy.wait_send()

    @pl.when(feeds)
    def _():
        for layer in range(layers):
            for dy in range(3):
                feed_copy(layer, dy).wait_send()

    @pl.when(feeds & (seg >= halfway))
    def _():
        second_own.wait_send()

    @pl.when(feeds & (seg < halfway))
    def _():
        first_mirror.wait_send()

    @pl.when(works & (seg < tail))
    def _():
        for copy in next_copies:
            copy.wait_send()

    @pl.when(works & (seg < halfway - 2))
    def _():
        for copy in skip_copies:
            copy.wait_send()

    @pl.when(works & (seg == tail))
    def _():
        for g in range(segments):
            for k in range(half_bands):
                if g != tail:
                    fin_copy(g, k).wait_send()
                else:

                    @pl.when(chunk_band(k) != band)
                    def _():
                        fin_copy(g, k).wait_send()


def shards(segments, bands, pixels, conv_weight, join_weight):
    batches, band_rows, columns, channels = pixels.shape
    layers = conv_weight.shape[1]
    own_rows = band_rows * bands // HALVES
    rows = own_rows + 2 * layers
    chunks = -(-rows // band_rows)
    own_px, halo_px, all_px = own_rows * columns, 2 * layers * columns, rows * columns
    mid_px = (own_rows + layers) * columns
    share = columns // segments
    piece = band_rows * share
    block_rows = -(-piece // 16) * 16
    blocks = segments * (bands // HALVES)
    workers = HALVES * batches
    kept = jnp.bfloat16
    conv = conv_weight.reshape(layers, 3, 3 * channels, channels)
    join = join_weight.reshape(channels, channels)
    dma = pltpu.SemaphoreType.DMA
    result = pl.pallas_call(
        functools.partial(kernel, segments, bands),
        out_shape=jax.ShapeDtypeStruct((batches, piece, channels), kept),
        in_specs=[pl.BlockSpec(memory_space=pltpu.HBM)] * 3,
        out_specs=pl.BlockSpec(memory_space=pltpu.VMEM),
        scratch_shapes=[
            pltpu.VMEM((chunks, band_rows, columns, channels), kept),
            pltpu.VMEM((all_px, channels), kept),
            pltpu.VMEM((all_px, channels), kept),
            pltpu.VMEM((mid_px, channels), kept),
            pltpu.VMEM((mid_px, channels), kept),
            pltpu.VMEM((2 * layers, 3, 3 * channels, channels), kept),
            pltpu.VMEM((2, channels, channels), kept),
            pltpu.VMEM((2, channels, channels), kept),
            pltpu.VMEM((all_px, channels), jnp.float32),
            pltpu.VMEM((all_px, channels), kept),
            pltpu.VMEM((all_px + columns, 3 * channels), kept),
            pltpu.VMEM((own_px, channels), kept),
            pltpu.VMEM((halo_px, channels), kept),
            pltpu.VMEM((blocks, block_rows, own_px), kept),
            pltpu.VMEM((blocks, block_rows, channels), kept),
            pltpu.VMEM((batches, block_rows, channels), kept),
            dma((layers, 3)),
            dma,
            dma((workers,)),
            dma((chunks,)),
            dma((2,)),
            dma((2,)),
            dma((2,)),
            dma((2,)),
            dma((3,)),
            dma((3,)),
            dma((layers, 3)),
            dma((layers, 3)),
            dma,
            dma,
            dma((blocks,)),
            dma((batches,)),
        ],
        compiler_params=pltpu.CompilerParams(collective_id=0, has_side_effects=True),
    )(pixels, conv, join)
    return result.reshape(batches, band_rows, share, channels)


def solution(mesh):
    return jax.shard_map(
        functools.partial(shards, mesh.shape["segment"], mesh.shape["band"]),
        mesh=mesh,
        in_specs=(
            P(None, "band", None, None),
            P("segment", None, None, None, None, None),
            P("segment", None, None),
        ),
        out_specs=P(None, "band", "segment", None),
        check_vma=False,
    )
```

```python
import functools

import jax
import jax.numpy as jnp
from jax import lax
from jax.experimental import pallas as pl
from jax.experimental.pallas import tpu as pltpu
from jax.sharding import PartitionSpec as P

MESH = pl.DeviceIdType.MESH
HALVES = 2


def unit(values):
    return values * lax.rsqrt(jnp.mean(values * values, axis=-1, keepdims=True) + 1e-05)


def kernel(
    segments,
    bands,
    pix_ref,
    conv_ref,
    join_ref,
    out_ref,
    pix_buf,
    in_buf,
    skip_buf,
    early_skip,
    early_out,
    weight_buf,
    own_join,
    mirror_join,
    skip_part,
    hid,
    wide,
    own_out,
    halo_out,
    place,
    fin_src,
    fin_dst,
    weight_sem,
    join_sem,
    pix_send,
    pix_recv,
    in_send,
    in_recv,
    skip_send,
    skip_recv,
    mirror_send,
    mirror_recv,
    feed_send,
    feed_recv,
    early_send,
    early_recv,
    fin_send,
    fin_recv,
):
    batches, band_rows, columns, channels = pix_ref.shape
    layers = conv_ref.shape[0]
    workers = HALVES * batches
    chunks = pix_buf.shape[0]
    own_px = own_out.shape[0]
    halo_px = halo_out.shape[0]
    all_px = own_px + halo_px
    half_bands = bands // HALVES
    halfway = segments // 2
    last = segments - 1
    tail = segments - 2
    share = columns // segments
    seg = lax.axis_index("segment")
    band = lax.axis_index("band")
    lower = lax.rem(band, HALVES)
    micro = lax.div(band, HALVES)
    other = band + 1 - 2 * lower
    works = (band < workers) & (lax.rem(seg, 2) == 0)
    feeds = (band < workers) & (lax.rem(seg, 2) == 1)
    own_half = lax.div(band, half_bands)

    weight_copies = []
    for layer in range(layers):
        for dy in range(3):
            to = dy + lower * (2 - 2 * dy)
            weight_copies.append(
                pltpu.make_async_copy(
                    conv_ref.at[layer, dy], weight_buf.at[layer, to], weight_sem.at[layer, dy]
                )
            )
    join_copy = pltpu.make_async_copy(join_ref, own_join.at[0], join_sem)

    @pl.when(works)
    def _():
        for copy in weight_copies:
            copy.start()
        join_copy.start()

    barrier = pltpu.get_barrier_semaphore()

    def greet(to_seg, to_band):
        pl.semaphore_signal(barrier, inc=1, device_id=(to_seg, to_band), device_id_type=MESH)

    def chunk_band(chunk):
        return chunk + lower * (bands - 1 - 2 * chunk)

    @pl.when(works & (seg == 0))
    def _():
        for chunk in range(chunks):

            @pl.when(chunk_band(chunk) != band)
            def _():
                greet(0, chunk_band(chunk))

    @pl.when(works)
    def _():
        greet(seg + 1, band)

    @pl.when(works & (seg > 0))
    def _():
        greet(seg - 2, band)
        greet(seg - 2, other)

    @pl.when(works & (seg > halfway))
    def _():
        greet(tail - seg, band)
        greet(tail - seg, other)

    @pl.when(works & (seg >= halfway))
    def _():
        greet(last - seg, band)

    for m in range(batches):

        @pl.when((seg != tail) | (band != HALVES * m + own_half))
        def _():
            greet(tail, HALVES * m + own_half)

    def one_if(condition):
        return jnp.where(condition, 1, 0).astype(jnp.int32)

    def pix_chunk(worker):
        return band if worker % HALVES == 0 else bands - 1 - band

    def pix_sends(worker):
        return (seg == 0) & (pix_chunk(worker) < chunks) & (band != worker)

    expected = one_if(works & (seg < tail)) * 2 + one_if(works & (seg < halfway - 2)) * 2
    expected += one_if(feeds) + one_if(feeds & (seg < halfway))
    for worker in range(workers):
        expected += one_if(pix_sends(worker))
    expected += one_if(works & (seg == tail)) * (
        segments * half_bands - one_if(own_half == lower)
    )

    @pl.when(expected > 0)
    def _():
        pl.semaphore_wait(barrier, expected)

    def pix_copy(worker):
        return pltpu.make_async_remote_copy(
            src_ref=pix_ref.at[worker // HALVES],
            dst_ref=pix_buf.at[pix_chunk(worker)],
            send_sem=pix_send.at[worker],
            recv_sem=pix_recv.at[pix_chunk(worker)],
            device_id=(0, worker),
            device_id_type=MESH,
        )

    own_chunk = band + lower * (bands - 1 - 2 * band)
    for worker in range(workers):

        @pl.when(pix_sends(worker))
        def _():
            pix_copy(worker).start()

    @pl.when(works & (seg == 0) & (own_chunk < chunks))
    def _():
        pltpu.make_async_copy(
            pix_ref.at[micro], pix_buf.at[own_chunk], pix_recv.at[own_chunk]
        ).start()

    def feed_copy(layer, dy):
        return pltpu.make_async_remote_copy(
            src_ref=conv_ref.at[layer, dy],
            dst_ref=weight_buf.at[layers + layer, dy + lower * (2 - 2 * dy)],
            send_sem=feed_send.at[layer, dy],
            recv_sem=feed_recv.at[layer, dy],
            device_id=(seg - 1, band),
            device_id_type=MESH,
        )

    def join_send(slot, to_seg, buffer, at):
        return pltpu.make_async_remote_copy(
            src_ref=join_ref,
            dst_ref=buffer.at[at],
            send_sem=mirror_send.at[slot],
            recv_sem=mirror_recv.at[slot],
            device_id=(to_seg, band),
            device_id_type=MESH,
        )

    second_own = join_send(0, seg - 1, own_join, 1)
    first_mirror = join_send(1, last - seg, mirror_join, 0)
    second_mirror = join_send(2, tail - seg, mirror_join, 1)

    @pl.when(feeds)
    def _():
        for layer in range(layers):
            for dy in range(3):
                feed_copy(layer, dy).start()

    @pl.when(feeds & (seg >= halfway))
    def _():
        second_own.start()

    @pl.when(feeds & (seg < halfway))
    def _():
        first_mirror.start()

    @pl.when(works & (seg < halfway))
    def _():
        second_mirror.start()

    early_copy = pltpu.make_async_remote_copy(
        src_ref=early_out,
        dst_ref=early_skip,
        send_sem=early_send,
        recv_sem=early_recv,
        device_id=(tail - seg, band),
        device_id_type=MESH,
    )

    def hop_copies(buffer, to_seg, send, recv):
        return (
            pltpu.make_async_remote_copy(
                src_ref=own_out,
                dst_ref=buffer.at[pl.ds(0, own_px)],
                send_sem=send.at[0],
                recv_sem=recv.at[0],
                device_id=(to_seg, band),
                device_id_type=MESH,
            ),
            pltpu.make_async_remote_copy(
                src_ref=halo_out,
                dst_ref=buffer.at[pl.ds(own_px, halo_px)],
                send_sem=send.at[1],
                recv_sem=recv.at[1],
                device_id=(to_seg, other),
                device_id_type=MESH,
            ),
        )

    next_copies = hop_copies(in_buf, seg + 2, in_send, in_recv)
    skip_copies = hop_copies(skip_buf, tail - seg, skip_send, skip_recv)

    def fin_copy(g, k):
        return pltpu.make_async_remote_copy(
            src_ref=fin_src.at[g * half_bands + k],
            dst_ref=fin_dst.at[micro],
            send_sem=fin_send.at[g * half_bands + k],
            recv_sem=fin_recv.at[micro],
            device_id=(g, chunk_band(k)),
            device_id_type=MESH,
        )

    def dot(a, b):
        return jnp.dot(a, b, preferred_element_type=jnp.float32)

    @pl.when(works)
    def _():
        @pl.when(seg == tail)
        def _():
            block_rows = fin_src.shape[1]
            at = lax.broadcasted_iota(jnp.int32, (block_rows, own_px), 0)
            pixel = lax.broadcasted_iota(jnp.int32, (block_rows, own_px), 1)
            row = jnp.zeros_like(at)
            for step in range(1, band_rows):
                row += jnp.where(at >= step * share, 1, 0)
            column = at - row * share
            row = row + lower * (band_rows - 1 - 2 * row)
            inside = at < band_rows * share
            base = row * columns + column
            for g in range(segments):
                for k in range(half_bands):
                    wanted = base + (k * band_rows * columns + g * share)
                    place[g * half_bands + k] = jnp.where(
                        inside & (pixel == wanted), 1.0, 0.0
                    ).astype(jnp.bfloat16)

        hid[...] = jnp.zeros_like(hid)
        wide[pl.ds(0, columns)] = jnp.zeros((columns, 3 * channels), jnp.bfloat16)
        join_copy.wait()

        @pl.when(seg > 0)
        def _():
            for copy in weight_copies:
                copy.wait()

        @pl.when(seg >= halfway)
        def _():
            first_mirror.wait_recv()
            second_mirror.wait_recv()
            second_own.wait_recv()

        @pl.when(seg > halfway)
        def _():
            for copy in skip_copies:
                copy.wait_recv()
            skip_part[...] = dot(skip_buf[...], mirror_join[0])

        def take_input():
            @pl.when(seg == 0)
            def _():
                for chunk in range(chunks):
                    pltpu.make_async_copy(
                        pix_ref.at[0], pix_buf.at[chunk], pix_recv.at[chunk]
                    ).wait()
                for row in range(all_px // columns):
                    within = row % band_rows
                    within = within + lower * (band_rows - 1 - 2 * within)
                    hid[pl.ds(row * columns, columns)] = pix_buf[row // band_rows, within]

            @pl.when(seg > 0)
            def _():
                for copy in next_copies:
                    copy.wait_recv()

            @pl.when((seg > 0) & (seg < halfway))
            def _():
                hid[...] = in_buf[...]

            @pl.when(seg == halfway)
            def _():
                skip_part[...] = dot(in_buf[...], mirror_join[0])

            @pl.when(seg >= halfway)
            def _():
                hid[...] = (skip_part[...] + dot(in_buf[...], own_join[0])).astype(jnp.bfloat16)

        def convolve(layer, count):
            keep = count - columns
            at = lax.broadcasted_iota(
                jnp.int32, (count // columns, columns, channels), 1
            ).reshape(count, channels)
            scaled = unit(hid[pl.ds(0, count)].astype(jnp.float32))
            left = jnp.where(at == 0, 0.0, pltpu.roll(scaled, 1, 0))
            right = jnp.where(at == columns - 1, 0.0, pltpu.roll(scaled, count - 1, 0))
            for dx, part in enumerate((left, scaled, right)):
                wide[pl.ds(columns, count), pl.ds(dx * channels, channels)] = part.astype(
                    jnp.bfloat16
                )
            total = dot(wide[pl.ds(0, keep)], weight_buf[layer, 0])
            for dy in range(1, 3):
                total += dot(wide[pl.ds(dy * columns, keep)], weight_buf[layer, dy])
            hid[pl.ds(0, keep)] = (
                hid[pl.ds(0, keep)].astype(jnp.float32) + jnp.maximum(total, 0.0)
            ).astype(jnp.bfloat16)

        mid_px = early_out.shape[0]

        def both_sections(turn, carry):
            real = turn == 1
            count = jnp.where(real, layers, 1)

            @pl.when(real)
            def _():
                take_input()

            def first_section(layer, inner):
                @pl.when((seg == 0) & (real == (layer > 0)))
                def _():
                    for dy in range(3):
                        pltpu.make_async_copy(
                            conv_ref.at[layer, dy],
                            weight_buf.at[layer, dy],
                            weight_sem.at[layer, dy],
                        ).wait()

                convolve(layer, all_px)
                return inner

            lax.fori_loop(0, count, first_section, 0)

            @pl.when(real & (seg < halfway))
            def _():
                early_out[...] = hid[pl.ds(0, mid_px)]
                early_copy.start()

            @pl.when(real & (seg >= halfway))
            def _():
                early_copy.wait_recv()
                hid[pl.ds(0, mid_px)] = (
                    dot(early_skip[...], mirror_join[1]) + dot(hid[pl.ds(0, mid_px)], own_join[1])
                ).astype(jnp.bfloat16)

            def second_section(layer, inner):
                @pl.when(real)
                def _():
                    for dy in range(3):
                        feed_copy(layer, dy).wait_recv()

                convolve(layer + jnp.where(real, layers, 0), mid_px)
                return inner

            lax.fori_loop(0, count, second_section, 0)
            return carry

        lax.fori_loop(0, 2, both_sections, 0)
        hidden = hid[pl.ds(0, own_px)]

        @pl.when(seg < tail)
        def _():
            for row in range(halo_px // columns):
                start = own_px - (row + 1) * columns
                halo_out[pl.ds(row * columns, columns)] = hidden[start : start + columns]
            own_out[...] = hidden
            for copy in next_copies[::-1]:
                copy.start()

            @pl.when(seg < halfway - 2)
            def _():
                for copy in skip_copies:
                    copy.start()

        @pl.when(seg == tail)
        def _():
            decoded = unit(hidden.astype(jnp.float32)).astype(jnp.bfloat16)
            sorting = place[...].reshape(-1, own_px)
            fin_src[...] = dot(sorting, decoded).astype(jnp.bfloat16).reshape(fin_src.shape)
            for g in range(segments):
                for k in range(half_bands):
                    if g != tail:
                        fin_copy(g, k).start()
                    else:
                        here = chunk_band(k) == band

                        @pl.when(here)
                        def _():
                            pltpu.make_async_copy(
                                fin_src.at[g * half_bands + k],
                                fin_dst.at[micro],
                                fin_recv.at[micro],
                            ).start()

                        @pl.when(jnp.logical_not(here))
                        def _():
                            fin_copy(g, k).start()

    for m in range(batches):
        pltpu.make_async_copy(fin_src.at[0], fin_dst.at[m], fin_recv.at[m]).wait()
    out_ref[...] = fin_dst[:, : out_ref.shape[1]]

    for worker in range(workers):

        @pl.when(pix_sends(worker))
        def _():
            pix_copy(worker).wait_send()

    @pl.when(works & (seg < halfway))
    def _():
        second_mirror.wait_send()
        early_copy.wait_send()

    @pl.when(feeds)
    def _():
        for layer in range(layers):
            for dy in range(3):
                feed_copy(layer, dy).wait_send()

    @pl.when(feeds & (seg >= halfway))
    def _():
        second_own.wait_send()

    @pl.when(feeds & (seg < halfway))
    def _():
        first_mirror.wait_send()

    @pl.when(works & (seg < tail))
    def _():
        for copy in next_copies:
            copy.wait_send()

    @pl.when(works & (seg < halfway - 2))
    def _():
        for copy in skip_copies:
            copy.wait_send()

    @pl.when(works & (seg == tail))
    def _():
        for g in range(segments):
            for k in range(half_bands):
                if g != tail:
                    fin_copy(g, k).wait_send()
                else:

                    @pl.when(chunk_band(k) != band)
                    def _():
                        fin_copy(g, k).wait_send()


def shards(segments, bands, pixels, conv_weight, join_weight):
    batches, band_rows, columns, channels = pixels.shape
    layers = conv_weight.shape[1]
    own_rows = band_rows * bands // HALVES
    rows = own_rows + 2 * layers
    chunks = -(-rows // band_rows)
    own_px, halo_px, all_px = own_rows * columns, 2 * layers * columns, rows * columns
    mid_px = (own_rows + layers) * columns
    share = columns // segments
    piece = band_rows * share
    block_rows = -(-piece // 16) * 16
    blocks = segments * (bands // HALVES)
    workers = HALVES * batches
    kept = jnp.bfloat16
    conv = conv_weight.reshape(layers, 3, 3 * channels, channels)
    join = join_weight.reshape(channels, channels)
    dma = pltpu.SemaphoreType.DMA
    result = pl.pallas_call(
        functools.partial(kernel, segments, bands),
        out_shape=jax.ShapeDtypeStruct((batches, piece, channels), kept),
        in_specs=[pl.BlockSpec(memory_space=pltpu.HBM)] * 3,
        out_specs=pl.BlockSpec(memory_space=pltpu.VMEM),
        scratch_shapes=[
            pltpu.VMEM((chunks, band_rows, columns, channels), kept),
            pltpu.VMEM((all_px, channels), kept),
            pltpu.VMEM((all_px, channels), kept),
            pltpu.VMEM((mid_px, channels), kept),
            pltpu.VMEM((mid_px, channels), kept),
            pltpu.VMEM((2 * layers, 3, 3 * channels, channels), kept),
            pltpu.VMEM((2, channels, channels), kept),
            pltpu.VMEM((2, channels, channels), kept),
            pltpu.VMEM((all_px, channels), jnp.float32),
            pltpu.VMEM((all_px, channels), kept),
            pltpu.VMEM((all_px + columns, 3 * channels), kept),
            pltpu.VMEM((own_px, channels), kept),
            pltpu.VMEM((halo_px, channels), kept),
            pltpu.VMEM((blocks, block_rows, own_px), kept),
            pltpu.VMEM((blocks, block_rows, channels), kept),
            pltpu.VMEM((batches, block_rows, channels), kept),
            dma((layers, 3)),
            dma,
            dma((workers,)),
            dma((chunks,)),
            dma((2,)),
            dma((2,)),
            dma((2,)),
            dma((2,)),
            dma((3,)),
            dma((3,)),
            dma((layers, 3)),
            dma((layers, 3)),
            dma,
            dma,
            dma((blocks,)),
            dma((batches,)),
        ],
        compiler_params=pltpu.CompilerParams(collective_id=0, has_side_effects=True),
    )(pixels, conv, join)
    return result.reshape(batches, band_rows, share, channels)


def solution(mesh):
    return jax.shard_map(
        functools.partial(shards, mesh.shape["segment"], mesh.shape["band"]),
        mesh=mesh,
        in_specs=(
            P(None, "band", None, None),
            P("segment", None, None, None, None, None),
            P("segment", None, None),
        ),
        out_specs=P(None, "band", "segment", None),
        check_vma=False,
    )
```

```python
import functools

import jax
import jax.numpy as jnp
from jax import lax
from jax.experimental import pallas as pl
from jax.experimental.pallas import tpu as pltpu
from jax.sharding import PartitionSpec as P

MESH = pl.DeviceIdType.MESH
HALVES = 2


def unit(values):
    return values * lax.rsqrt(jnp.mean(values * values, axis=-1, keepdims=True) + 1e-05)


def kernel(
    segments,
    bands,
    pix_ref,
    conv_ref,
    join_ref,
    out_ref,
    pix_buf,
    in_buf,
    skip_buf,
    early_skip,
    early_out,
    weight_buf,
    own_join,
    mirror_join,
    skip_part,
    hid,
    wide,
    own_out,
    halo_out,
    place,
    fin_src,
    fin_dst,
    weight_sem,
    join_sem,
    pix_send,
    pix_recv,
    in_send,
    in_recv,
    skip_send,
    skip_recv,
    mirror_send,
    mirror_recv,
    feed_send,
    feed_recv,
    early_send,
    early_recv,
    fin_send,
    fin_recv,
):
    batches, band_rows, columns, channels = pix_ref.shape
    layers = conv_ref.shape[0]
    workers = HALVES * batches
    chunks = pix_buf.shape[0]
    own_px = own_out.shape[0]
    halo_px = halo_out.shape[0]
    all_px = own_px + halo_px
    half_bands = bands // HALVES
    halfway = segments // 2
    last = segments - 1
    tail = segments - 2
    share = columns // segments
    seg = lax.axis_index("segment")
    band = lax.axis_index("band")
    lower = lax.rem(band, HALVES)
    micro = lax.div(band, HALVES)
    other = band + 1 - 2 * lower
    works = (band < workers) & (lax.rem(seg, 2) == 0)
    feeds = (band < workers) & (lax.rem(seg, 2) == 1)
    own_half = lax.div(band, half_bands)

    weight_copies = []
    for layer in range(layers):
        for dy in range(3):
            to = dy + lower * (2 - 2 * dy)
            weight_copies.append(
                pltpu.make_async_copy(
                    conv_ref.at[layer, dy], weight_buf.at[layer, to], weight_sem.at[layer, dy]
                )
            )
    join_copy = pltpu.make_async_copy(join_ref, own_join.at[0], join_sem)

    @pl.when(works)
    def _():
        for copy in weight_copies:
            copy.start()
        join_copy.start()

    barrier = pltpu.get_barrier_semaphore()

    def greet(to_seg, to_band):
        pl.semaphore_signal(barrier, inc=1, device_id=(to_seg, to_band), device_id_type=MESH)

    def chunk_band(chunk):
        return chunk + lower * (bands - 1 - 2 * chunk)

    @pl.when(works & (seg == 0))
    def _():
        for chunk in range(chunks):

            @pl.when(chunk_band(chunk) != band)
            def _():
                greet(0, chunk_band(chunk))

    @pl.when(works)
    def _():
        greet(seg + 1, band)

    @pl.when(works & (seg > 0))
    def _():
        greet(seg - 2, band)
        greet(seg - 2, other)

    @pl.when(works & (seg > halfway))
    def _():
        greet(tail - seg, band)
        greet(tail - seg, other)

    @pl.when(works & (seg >= halfway))
    def _():
        greet(last - seg, band)

    for m in range(batches):

        @pl.when((seg != tail) | (band != HALVES * m + own_half))
        def _():
            greet(tail, HALVES * m + own_half)

    def one_if(condition):
        return jnp.where(condition, 1, 0).astype(jnp.int32)

    def pix_chunk(worker):
        return band if worker % HALVES == 0 else bands - 1 - band

    def pix_sends(worker):
        return (seg == 0) & (pix_chunk(worker) < chunks) & (band != worker)

    expected = one_if(works & (seg < tail)) * 2 + one_if(works & (seg < halfway - 2)) * 2
    expected += one_if(feeds) + one_if(feeds & (seg < halfway))
    for worker in range(workers):
        expected += one_if(pix_sends(worker))
    expected += one_if(works & (seg == tail)) * (
        segments * half_bands - one_if(own_half == lower)
    )

    @pl.when(expected > 0)
    def _():
        pl.semaphore_wait(barrier, expected)

    def pix_copy(worker):
        return pltpu.make_async_remote_copy(
            src_ref=pix_ref.at[worker // HALVES],
            dst_ref=pix_buf.at[pix_chunk(worker)],
            send_sem=pix_send.at[worker],
            recv_sem=pix_recv.at[pix_chunk(worker)],
            device_id=(0, worker),
            device_id_type=MESH,
        )

    own_chunk = band + lower * (bands - 1 - 2 * band)
    for worker in range(workers):

        @pl.when(pix_sends(worker))
        def _():
            pix_copy(worker).start()

    @pl.when(works & (seg == 0) & (own_chunk < chunks))
    def _():
        pltpu.make_async_copy(
            pix_ref.at[micro], pix_buf.at[own_chunk], pix_recv.at[own_chunk]
        ).start()

    def feed_copy(layer, dy):
        return pltpu.make_async_remote_copy(
            src_ref=conv_ref.at[layer, dy],
            dst_ref=weight_buf.at[layers + layer, dy + lower * (2 - 2 * dy)],
            send_sem=feed_send.at[layer, dy],
            recv_sem=feed_recv.at[layer, dy],
            device_id=(seg - 1, band),
            device_id_type=MESH,
        )

    def join_send(slot, to_seg, buffer, at):
        return pltpu.make_async_remote_copy(
            src_ref=join_ref,
            dst_ref=buffer.at[at],
            send_sem=mirror_send.at[slot],
            recv_sem=mirror_recv.at[slot],
            device_id=(to_seg, band),
            device_id_type=MESH,
        )

    second_own = join_send(0, seg - 1, own_join, 1)
    first_mirror = join_send(1, last - seg, mirror_join, 0)
    second_mirror = join_send(2, tail - seg, mirror_join, 1)

    @pl.when(feeds)
    def _():
        for layer in range(layers):
            for dy in range(3):
                feed_copy(layer, dy).start()

    @pl.when(feeds & (seg >= halfway))
    def _():
        second_own.start()

    @pl.when(feeds & (seg < halfway))
    def _():
        first_mirror.start()

    @pl.when(works & (seg < halfway))
    def _():
        second_mirror.start()

    early_copy = pltpu.make_async_remote_copy(
        src_ref=early_out,
        dst_ref=early_skip,
        send_sem=early_send,
        recv_sem=early_recv,
        device_id=(tail - seg, band),
        device_id_type=MESH,
    )

    def hop_copies(buffer, to_seg, send, recv):
        return (
            pltpu.make_async_remote_copy(
                src_ref=hid.at[pl.ds(0, own_px)],
                dst_ref=buffer.at[pl.ds(0, own_px)],
                send_sem=send.at[0],
                recv_sem=recv.at[0],
                device_id=(to_seg, band),
                device_id_type=MESH,
            ),
            pltpu.make_async_remote_copy(
                src_ref=halo_out,
                dst_ref=buffer.at[pl.ds(own_px, halo_px)],
                send_sem=send.at[1],
                recv_sem=recv.at[1],
                device_id=(to_seg, other),
                device_id_type=MESH,
            ),
        )

    next_copies = hop_copies(in_buf, seg + 2, in_send, in_recv)
    skip_copies = hop_copies(skip_buf, tail - seg, skip_send, skip_recv)

    def fin_copy(g, k):
        return pltpu.make_async_remote_copy(
            src_ref=fin_src.at[g * half_bands + k],
            dst_ref=fin_dst.at[micro],
            send_sem=fin_send.at[g * half_bands + k],
            recv_sem=fin_recv.at[micro],
            device_id=(g, chunk_band(k)),
            device_id_type=MESH,
        )

    def dot(a, b):
        return jnp.dot(a, b, preferred_element_type=jnp.float32)

    @pl.when(works)
    def _():
        @pl.when(seg == tail)
        def _():
            block_rows = fin_src.shape[1]
            at = lax.broadcasted_iota(jnp.int32, (block_rows, own_px), 0)
            pixel = lax.broadcasted_iota(jnp.int32, (block_rows, own_px), 1)
            row = jnp.zeros_like(at)
            for step in range(1, band_rows):
                row += jnp.where(at >= step * share, 1, 0)
            column = at - row * share
            row = row + lower * (band_rows - 1 - 2 * row)
            inside = at < band_rows * share
            base = row * columns + column
            for g in range(segments):
                for k in range(half_bands):
                    wanted = base + (k * band_rows * columns + g * share)
                    place[g * half_bands + k] = jnp.where(
                        inside & (pixel == wanted), 1.0, 0.0
                    ).astype(jnp.bfloat16)

        hid[...] = jnp.zeros_like(hid)
        wide[pl.ds(0, columns)] = jnp.zeros((columns, 3 * channels), jnp.bfloat16)
        join_copy.wait()

        @pl.when(seg > 0)
        def _():
            for copy in weight_copies:
                copy.wait()

        @pl.when(seg >= halfway)
        def _():
            first_mirror.wait_recv()
            second_mirror.wait_recv()
            second_own.wait_recv()

        @pl.when(seg > halfway)
        def _():
            for copy in skip_copies:
                copy.wait_recv()
            skip_part[...] = dot(skip_buf[...], mirror_join[0])

        def take_input():
            @pl.when(seg == 0)
            def _():
                for chunk in range(chunks):
                    pltpu.make_async_copy(
                        pix_ref.at[0], pix_buf.at[chunk], pix_recv.at[chunk]
                    ).wait()
                for row in range(all_px // columns):
                    within = row % band_rows
                    within = within + lower * (band_rows - 1 - 2 * within)
                    hid[pl.ds(row * columns, columns)] = pix_buf[row // band_rows, within]

            @pl.when(seg > 0)
            def _():
                for copy in next_copies:
                    copy.wait_recv()

            @pl.when((seg > 0) & (seg < halfway))
            def _():
                hid[...] = in_buf[...]

            @pl.when(seg == halfway)
            def _():
                skip_part[...] = dot(in_buf[...], mirror_join[0])

            @pl.when(seg >= halfway)
            def _():
                hid[...] = (skip_part[...] + dot(in_buf[...], own_join[0])).astype(jnp.bfloat16)

        def convolve(layer, count):
            keep = count - columns
            at = lax.broadcasted_iota(
                jnp.int32, (count // columns, columns, channels), 1
            ).reshape(count, channels)
            scaled = unit(hid[pl.ds(0, count)].astype(jnp.float32))
            left = jnp.where(at == 0, 0.0, pltpu.roll(scaled, 1, 0))
            right = jnp.where(at == columns - 1, 0.0, pltpu.roll(scaled, count - 1, 0))
            for dx, part in enumerate((left, scaled, right)):
                wide[pl.ds(columns, count), pl.ds(dx * channels, channels)] = part.astype(
                    jnp.bfloat16
                )
            total = dot(wide[pl.ds(0, keep)], weight_buf[layer, 0])
            for dy in range(1, 3):
                total += dot(wide[pl.ds(dy * columns, keep)], weight_buf[layer, dy])
            hid[pl.ds(0, keep)] = (
                hid[pl.ds(0, keep)].astype(jnp.float32) + jnp.maximum(total, 0.0)
            ).astype(jnp.bfloat16)

        mid_px = early_out.shape[0]

        def both_sections(turn, carry):
            real = turn == 1
            count = jnp.where(real, layers, 1)

            @pl.when(real)
            def _():
                take_input()

            def first_section(layer, inner):
                @pl.when(seg == 0)
                def _():
                    for dy in range(3):
                        pltpu.make_async_copy(
                            conv_ref.at[layer, dy],
                            weight_buf.at[layer, dy],
                            weight_sem.at[layer, dy],
                        ).wait()

                convolve(layer, all_px)
                return inner

            lax.fori_loop(0, count, first_section, 0)

            @pl.when(real & (seg < halfway))
            def _():
                early_out[...] = hid[pl.ds(0, mid_px)]
                early_copy.start()

            @pl.when(real & (seg >= halfway))
            def _():
                early_copy.wait_recv()
                hid[pl.ds(0, mid_px)] = (
                    dot(early_skip[...], mirror_join[1]) + dot(hid[pl.ds(0, mid_px)], own_join[1])
                ).astype(jnp.bfloat16)

            def second_section(layer, inner):
                @pl.when(real)
                def _():
                    for dy in range(3):
                        feed_copy(layer, dy).wait_recv()

                convolve(layer + jnp.where(real, layers, 0), mid_px)
                return inner

            lax.fori_loop(0, count, second_section, 0)
            return carry

        lax.fori_loop(one_if(seg == 0), 2, both_sections, 0)
        hidden = hid[pl.ds(0, own_px)]

        @pl.when(seg < tail)
        def _():
            for row in range(halo_px // columns):
                start = own_px - (row + 1) * columns
                halo_out[pl.ds(row * columns, columns)] = hidden[start : start + columns]
            for copy in next_copies[::-1]:
                copy.start()

            @pl.when(seg < halfway - 2)
            def _():
                for copy in skip_copies:
                    copy.start()

        @pl.when(seg == tail)
        def _():
            decoded = unit(hidden.astype(jnp.float32)).astype(jnp.bfloat16)
            sorting = place[...].reshape(-1, own_px)
            fin_src[...] = dot(sorting, decoded).astype(jnp.bfloat16).reshape(fin_src.shape)
            for g in range(segments):
                for k in range(half_bands):
                    if g != tail:
                        fin_copy(g, k).start()
                    else:
                        here = chunk_band(k) == band

                        @pl.when(here)
                        def _():
                            pltpu.make_async_copy(
                                fin_src.at[g * half_bands + k],
                                fin_dst.at[micro],
                                fin_recv.at[micro],
                            ).start()

                        @pl.when(jnp.logical_not(here))
                        def _():
                            fin_copy(g, k).start()

    for m in range(batches):
        pltpu.make_async_copy(fin_src.at[0], fin_dst.at[m], fin_recv.at[m]).wait()
    out_ref[...] = fin_dst[:, : out_ref.shape[1]]

    for worker in range(workers):

        @pl.when(pix_sends(worker))
        def _():
            pix_copy(worker).wait_send()

    @pl.when(works & (seg < halfway))
    def _():
        second_mirror.wait_send()
        early_copy.wait_send()

    @pl.when(feeds)
    def _():
        for layer in range(layers):
            for dy in range(3):
                feed_copy(layer, dy).wait_send()

    @pl.when(feeds & (seg >= halfway))
    def _():
        second_own.wait_send()

    @pl.when(feeds & (seg < halfway))
    def _():
        first_mirror.wait_send()

    @pl.when(works & (seg < tail))
    def _():
        for copy in next_copies:
            copy.wait_send()

    @pl.when(works & (seg < halfway - 2))
    def _():
        for copy in skip_copies:
            copy.wait_send()

    @pl.when(works & (seg == tail))
    def _():
        for g in range(segments):
            for k in range(half_bands):
                if g != tail:
                    fin_copy(g, k).wait_send()
                else:

                    @pl.when(chunk_band(k) != band)
                    def _():
                        fin_copy(g, k).wait_send()


def shards(segments, bands, pixels, conv_weight, join_weight):
    batches, band_rows, columns, channels = pixels.shape
    layers = conv_weight.shape[1]
    own_rows = band_rows * bands // HALVES
    rows = own_rows + 2 * layers
    chunks = -(-rows // band_rows)
    own_px, halo_px, all_px = own_rows * columns, 2 * layers * columns, rows * columns
    mid_px = (own_rows + layers) * columns
    share = columns // segments
    piece = band_rows * share
    block_rows = -(-piece // 16) * 16
    blocks = segments * (bands // HALVES)
    workers = HALVES * batches
    kept = jnp.bfloat16
    conv = conv_weight.reshape(layers, 3, 3 * channels, channels)
    join = join_weight.reshape(channels, channels)
    dma = pltpu.SemaphoreType.DMA
    result = pl.pallas_call(
        functools.partial(kernel, segments, bands),
        out_shape=jax.ShapeDtypeStruct((batches, piece, channels), kept),
        in_specs=[pl.BlockSpec(memory_space=pltpu.HBM)] * 3,
        out_specs=pl.BlockSpec(memory_space=pltpu.VMEM),
        scratch_shapes=[
            pltpu.VMEM((chunks, band_rows, columns, channels), kept),
            pltpu.VMEM((all_px, channels), kept),
            pltpu.VMEM((all_px, channels), kept),
            pltpu.VMEM((mid_px, channels), kept),
            pltpu.VMEM((mid_px, channels), kept),
            pltpu.VMEM((2 * layers, 3, 3 * channels, channels), kept),
            pltpu.VMEM((2, channels, channels), kept),
            pltpu.VMEM((2, channels, channels), kept),
            pltpu.VMEM((all_px, channels), jnp.float32),
            pltpu.VMEM((all_px, channels), kept),
            pltpu.VMEM((all_px + columns, 3 * channels), kept),
            pltpu.VMEM((own_px, channels), kept),
            pltpu.VMEM((halo_px, channels), kept),
            pltpu.VMEM((blocks, block_rows, own_px), kept),
            pltpu.VMEM((blocks, block_rows, channels), kept),
            pltpu.VMEM((batches, block_rows, channels), kept),
            dma((layers, 3)),
            dma,
            dma((workers,)),
            dma((chunks,)),
            dma((2,)),
            dma((2,)),
            dma((2,)),
            dma((2,)),
            dma((3,)),
            dma((3,)),
            dma((layers, 3)),
            dma((layers, 3)),
            dma,
            dma,
            dma((blocks,)),
            dma((batches,)),
        ],
        compiler_params=pltpu.CompilerParams(collective_id=0, has_side_effects=True),
    )(pixels, conv, join)
    return result.reshape(batches, band_rows, share, channels)


def solution(mesh):
    return jax.shard_map(
        functools.partial(shards, mesh.shape["segment"], mesh.shape["band"]),
        mesh=mesh,
        in_specs=(
            P(None, "band", None, None),
            P("segment", None, None, None, None, None),
            P("segment", None, None),
        ),
        out_specs=P(None, "band", "segment", None),
        check_vma=False,
    )
```
